32 devices in a mesh: dp: 4 (over z), seq: 8 (over y, x, core).
Axes of the slice: x: 2, y: 2, z: 4, core: 2. Of those that a mesh axis runs over, the one named last changes fastest.
Arguments:
- tokens: bfloat16 [4, 3072, 4096], P('dp', 'seq'), may hold values from -16 to 16
- qkv_weight: bfloat16 [4096, 3072], P(('dp', 'seq')), may hold values from -1 to 1
- segments: int32 [4, 3072], P('dp', 'seq'), may hold values from 0 to 3071, as said below
- destination: int32 [4, 3072], P('dp', 'seq'), may hold values from 0 to 3071, as said below
- doc_prefix: int32 [4, 8], P('dp', 'seq'), may hold values from 0 to 768, as said below
Outputs:
- attended: bfloat16 [4, 3072, 2048], P('dp', 'seq')
The draws below stay inside these ranges and needn't reach their ends.
Inputs may be any that keep to these rules, and one draw needn't show every extreme that they name: `segments`: A token's id is the position in its sequence of its document's first token, so ids never fall and start at 0; the last token of every sequence is a document of its own. doc_prefix[b, d] is the number of tokens before row d * 384 of sequence b with that row's segment id; the most is reached in every draw. `destination`: each row is a permutation; the tokens of one device go to exactly 8 devices of the sequence, exactly 48 to each, and every device receives tokens from exactly 8 devices.
All inputs are finite; a program needn't handle non-finite values.
Results may differ from the reference program's by a relative error of at most 0.012.
The reference program's roundings to bfloat16 on the way (of `probs` and `heads_out`) count: a program that leaves them out, or rounds other values in their place, can miss the bound.
Values may be sent and summed in bfloat16 or wider, within the bound.
A program may use at most 128 MiB of HBM per device.

```python
import jax
import jax.numpy as jnp
from jax import lax

D = 4096
HEADS = 16
KV_HEADS = 4
HEAD_DIM = 128
TOK_DEV = 384
REACH = 2
GROUPS = 8
CAP = 48
SEQ_LEN = 3072
BATCH = 4
QKV = 3072
N_SEQ = 8


def document_flags(key):

    def draw_row(row_key):
        subkeys = jax.random.split(row_key, 3)
        index_list = jnp.arange(SEQ_LEN, dtype=jnp.int32)
        doc_flags = jax.random.randint(subkeys[0], (SEQ_LEN,), 0, 48) == 0
        anchor = jax.random.randint(subkeys[1], (), 0, N_SEQ - REACH)
        tail_len = jax.random.randint(subkeys[2], (), 1, TOK_DEV)
        device = index_list // TOK_DEV
        at_start = index_list % TOK_DEV == 0
        forced = at_start & ((device - anchor) % REACH == 0)
        doc_flags = doc_flags | forced | (index_list == 0)
        lower = anchor * TOK_DEV
        upper = (anchor + REACH) * TOK_DEV + tail_len
        doc_flags = jnp.where((index_list > lower) & (index_list < upper), False, doc_flags)
        return doc_flags | (index_list == lower) | (index_list == upper) | (index_list == SEQ_LEN - 1)
    return jax.vmap(draw_row)(jax.random.split(key, BATCH))


def document_starts(doc_flags):
    index_list = jnp.arange(SEQ_LEN, dtype=jnp.int32)
    return lax.cummax(jnp.where(doc_flags, index_list[None, :], 0), axis=1).astype(jnp.int32)


def draw_segments(key, part):
    doc_flags = document_flags(jax.random.fold_in(key, 11))
    return document_starts(doc_flags)


def draw_doc_prefix(key, part):
    doc_flags = document_flags(jax.random.fold_in(key, 11))
    doc_start = document_starts(doc_flags)
    starts = doc_start[:, ::TOK_DEV]
    return (jnp.arange(N_SEQ, dtype=jnp.int32)[None, :] * TOK_DEV - starts).astype(jnp.int32)


def draw_destination(key, part):

    def draw_row(row_key):
        subkeys = jax.random.split(row_key, 4)
        relabel = jax.random.permutation(subkeys[0], N_SEQ)
        inverse = jnp.argsort(relabel)
        shifts = jax.random.permutation(subkeys[1], N_SEQ)[:GROUPS]
        source_perm = jax.vmap(lambda inner: jax.random.permutation(inner, TOK_DEV))(jax.random.split(subkeys[2], N_SEQ))
        target_perm = jax.vmap(lambda inner: jax.random.permutation(inner, TOK_DEV))(jax.random.split(subkeys[3], N_SEQ))
        device = jnp.arange(N_SEQ, dtype=jnp.int32)[:, None]
        block_index = source_perm // CAP
        offset = source_perm % CAP
        target = inverse[(relabel[device] + shifts[block_index]) % N_SEQ]
        target_row = target_perm[target, block_index * CAP + offset]
        return (target * TOK_DEV + target_row).reshape(SEQ_LEN).astype(jnp.int32)
    return jax.vmap(draw_row)(jax.random.split(jax.random.fold_in(key, 41), BATCH))


def draw_tokens(key, part):
    subkeys = jax.random.split(jax.random.fold_in(key, 21), 1)
    values = jax.random.normal(subkeys[0], (BATCH, SEQ_LEN, D))
    return jnp.clip(values, -16.0, 16.0).astype(jnp.bfloat16)


def draw_qkv_weight(key, part):
    subkeys = jax.random.split(jax.random.fold_in(key, 31), 1)
    values = jax.random.normal(subkeys[0], (D, QKV)) * D ** (-0.5)
    return jnp.clip(values, -1.0, 1.0).astype(jnp.bfloat16)


def setup_inputs(seed: int = 0) -> dict:
    keys = jax.random.split(jax.random.key(seed), 6)
    tokens = draw_tokens(jax.random.fold_in(keys[5], 71), 0)
    qkv_weight = draw_qkv_weight(jax.random.fold_in(keys[5], 71), 0)
    segments = draw_segments(jax.random.fold_in(keys[5], 71), 0)
    destination = draw_destination(jax.random.fold_in(keys[5], 71), 0)
    doc_prefix = draw_doc_prefix(jax.random.fold_in(keys[5], 71), 0)
    return dict(tokens=tokens, qkv_weight=qkv_weight, segments=segments, destination=destination, doc_prefix=doc_prefix)


ROPE_BASE = 500000.0
MASKED = -1.0e30


def positions(segment_ids, prefix_len):
    index_list = jnp.arange(segment_ids.shape[0], dtype=jnp.int32)
    fresh_doc = jnp.concatenate([jnp.ones((1,), jnp.bool_), segment_ids[1:] != segment_ids[:-1]])
    first_row = lax.cummax(jnp.where(fresh_doc, index_list, 0), axis=0)
    leading = segment_ids == segment_ids[0]
    position = index_list - first_row + jnp.where(leading, prefix_len, 0)
    return position, leading


def rotate(heads, position):
    half_dim = heads.shape[-1] // 2
    frequency = ROPE_BASE ** (-2.0 * jnp.arange(half_dim, dtype=jnp.float32) / heads.shape[-1])
    angles = position.astype(jnp.float32)[:, None] * frequency[None, :]
    cosine = jnp.cos(angles)[:, None, :]
    sine = jnp.sin(angles)[:, None, :]
    first_half = heads[..., :half_dim]
    second_half = heads[..., half_dim:]
    return jnp.concatenate([first_half * cosine - second_half * sine, second_half * cosine + first_half * sine], axis=-1)


def visible_keys(segment_ids, leading, prefix_len, reach):
    count = segment_ids.shape[0]
    query_rows = jnp.arange(count, dtype=jnp.int32)
    columns = jnp.arange((reach + 1) * count, dtype=jnp.int32) - reach * count
    key_segments = jnp.concatenate([jnp.full((reach * count,), -1, jnp.int32), segment_ids])
    local_part = (columns[None, :] >= 0) & (columns[None, :] <= query_rows[:, None]) & (key_segments[None, :] == segment_ids[:, None])
    remote_part = (columns[None, :] < 0) & (columns[None, :] >= -prefix_len) & leading[:, None]
    return local_part | remote_part


def attend(queries, keys_rot, values, key_mask):
    query_f = queries.astype(jnp.float32)
    key_f = keys_rot.astype(jnp.float32)
    value_f = values.astype(jnp.float32)
    scores = jnp.einsum("tkgd,lkd->kgtl", query_f, key_f) * (HEAD_DIM ** -0.5)
    scores = jnp.where(key_mask[None, None], scores, MASKED)
    top_score = jnp.max(scores, axis=-1, keepdims=True)
    expo = jnp.exp(scores - top_score)
    row_total = jnp.sum(expo, axis=-1, keepdims=True)
    probs = (expo / row_total).astype(jnp.bfloat16)
    heads_out = jnp.einsum("kgtl,lkd->tkgd", probs.astype(jnp.float32), value_f)
    return heads_out.reshape(queries.shape[0], HEADS * HEAD_DIM).astype(jnp.bfloat16)


def one_sequence(weight, packed):
    token_rows, segment_row, target_row, prefix_row = packed
    query_width = HEADS * HEAD_DIM
    kv_width = KV_HEADS * HEAD_DIM
    group_size = HEADS // KV_HEADS
    projected = jnp.dot(token_rows, weight, preferred_element_type=jnp.float32)
    position, leading = jax.vmap(positions)(segment_row.reshape(N_SEQ, TOK_DEV), prefix_row)
    position = position.reshape(SEQ_LEN)
    leading = leading.reshape(SEQ_LEN)
    queries = rotate(projected[:, :query_width].reshape(SEQ_LEN, HEADS, HEAD_DIM), position).astype(jnp.bfloat16)
    keys_rot = rotate(projected[:, query_width:query_width + kv_width].reshape(SEQ_LEN, KV_HEADS, HEAD_DIM), position).astype(jnp.bfloat16)
    values = projected[:, query_width + kv_width:].reshape(SEQ_LEN, KV_HEADS, HEAD_DIM).astype(jnp.bfloat16)
    front_pad = REACH * TOK_DEV
    keys_pad = jnp.concatenate([jnp.zeros((front_pad, KV_HEADS, HEAD_DIM), jnp.bfloat16), keys_rot], axis=0)
    values_pad = jnp.concatenate([jnp.zeros((front_pad, KV_HEADS, HEAD_DIM), jnp.bfloat16), values], axis=0)

    def per_device(device):
        row_start = (device * TOK_DEV).astype(jnp.int32)
        query_block = lax.dynamic_slice_in_dim(queries, row_start, TOK_DEV, 0).reshape(TOK_DEV, KV_HEADS, group_size, HEAD_DIM)
        key_block = lax.dynamic_slice_in_dim(keys_pad, row_start, front_pad + TOK_DEV, 0)
        value_block = lax.dynamic_slice_in_dim(values_pad, row_start, front_pad + TOK_DEV, 0)
        segment_block = lax.dynamic_slice_in_dim(segment_row, row_start, TOK_DEV, 0)
        leading_block = lax.dynamic_slice_in_dim(leading, row_start, TOK_DEV, 0)
        key_mask = visible_keys(segment_block, leading_block, prefix_row[device], REACH)
        return attend(query_block, key_block, value_block, key_mask)

    heads_out = lax.map(per_device, jnp.arange(N_SEQ, dtype=jnp.int32)).reshape(SEQ_LEN, query_width)
    return jnp.zeros_like(heads_out).at[target_row].set(heads_out)


def reference(tokens, qkv_weight, segments, destination, doc_prefix):
    def run_one(packed):
        return one_sequence(qkv_weight, packed)

    return lax.map(run_one, (tokens, segments, destination, doc_prefix))
```

```python
import functools

import jax
import jax.numpy as jnp
from jax import lax
from jax.experimental import pallas as pl
from jax.experimental.pallas import tpu as pltpu
from jax.sharding import PartitionSpec as P

HEADS = 16
KV_HEADS = 4
HEAD_DIM = 128
REACH = 2
ROPE_BASE = 500000.0
MASKED = -1e30
CORES = 2
MESH = pl.DeviceIdType.MESH
META_ROWS = 8

ORDERS = ("zyx", "zxy", "xyz")


def part_bounds(width):
    unit = width // 12
    return ((0, 5 * unit), (5 * unit, 4 * unit), (9 * unit, 3 * unit))


def forwards(order, offset, depth):
    delta = dict(zip("xyz", offset))
    last = max([order.index(a) for a in order if delta[a]], default=-1)
    hops = []
    for index, axis in enumerate(order):
        if index < last:
            continue
        if axis == "z":
            steps = (1, -1) if delta["z"] == 0 else ((1,) if delta["z"] < 0 else (-1,))
            for step in steps:
                if abs(delta["z"] - step) < depth:
                    hops.append(("z", step, (delta["x"], delta["y"], delta["z"] - step)))
        elif index > last:
            there = dict(delta)
            there[axis] = 1
            hops.append((axis, 1, (there["x"], there["y"], there["z"])))
    return hops


def project_kernel(depth, n_seq, tok_ref, w_ref, meta_ref, out_ref, meta_out,
                   tok_all, w_all, meta_all, local_sem, pair_send, pair_recv,
                   meta_send, meta_recv, block_send, block_recv):
    z = lax.axis_index("dp")
    seq = lax.axis_index("seq")
    core = lax.rem(seq, CORES)
    plane = seq // CORES
    x = lax.rem(plane, 2)
    y = plane // 2
    rows, model = tok_ref.shape
    shard = w_ref.shape[0]
    half = out_ref.shape[1]
    heads_per = HEADS // CORES * HEAD_DIM
    kv_per = KV_HEADS // CORES * HEAD_DIM
    block_rows = shard * CORES
    partner = (z, seq + 1 - 2 * core)
    side = {
        "x": (z, (y * 2 + 1 - x) * CORES + core),
        "y": (z, ((1 - y) * 2 + x) * CORES + core),
    }

    def inside(dz):
        return (z + dz >= 0) & (z + dz < depth)

    barrier = pltpu.get_barrier_semaphore()
    for step in range(1, n_seq):
        pl.semaphore_signal(barrier, inc=1, device_id=(z, lax.rem(seq + step, n_seq)),
                            device_id_type=MESH)
    for step in (1, -1):
        @pl.when(inside(step))
        def _(step=step):
            pl.semaphore_signal(barrier, inc=1, device_id=(z + step, seq), device_id_type=MESH)
    peers = n_seq - 1 + jnp.where(z > 0, 1, 0) + jnp.where(z < depth - 1, 1, 0)
    pl.semaphore_wait(barrier, peers)

    def chip_of(offset):
        dx, dy, dz = offset
        cx = 1 - x if dx else x
        cy = 1 - y if dy else y
        return ((z + dz) * 2 + cy) * 2 + cx

    mine = chip_of((0, 0, 0))
    own_rows = pl.ds(pl.multiple_of(core * shard, shard), shard)
    slices = ((0, 0, heads_per), (HEADS * HEAD_DIM, heads_per, kv_per),
              ((HEADS + KV_HEADS) * HEAD_DIM, heads_per + kv_per, kv_per))
    first = []
    for index, (base, place, width) in enumerate(slices):
        there = pl.ds(pl.multiple_of(base + (1 - core) * width, 128), width)
        here = pl.ds(pl.multiple_of(base + core * width, 128), width)
        first.append(pltpu.make_async_remote_copy(
            src_ref=w_ref.at[:, there], dst_ref=w_all.at[mine, own_rows, pl.ds(place, width)],
            send_sem=pair_send.at[index], recv_sem=pair_recv.at[index],
            device_id=partner, device_id_type=MESH))
        first.append(pltpu.make_async_copy(
            w_ref.at[:, here], w_all.at[mine, own_rows, pl.ds(place, width)],
            local_sem.at[index]))
    for copy in first:
        copy.start()
    tok_rows = pl.ds(pl.multiple_of(core * rows, rows), rows)
    tok_send = pltpu.make_async_remote_copy(
        src_ref=tok_ref, dst_ref=tok_all.at[tok_rows, :], send_sem=pair_send.at[3],
        recv_sem=pair_recv.at[3], device_id=partner, device_id_type=MESH)
    tok_copy = pltpu.make_async_copy(tok_ref, tok_all.at[tok_rows, :], local_sem.at[3])
    for copy in first:
        copy.wait()

    ids = {}
    pending = []

    def block(part, offset):
        start, width = part_bounds(half)[part]
        return w_all.at[chip_of(offset), :, pl.ds(start, width)]

    def recv_index(part, offset):
        dx, dy, dz = offset
        return ((part * (2 * depth - 1) + dz + depth - 1) * 2 + dy) * 2 + dx

    def send(part, offset, hop):
        axis, step, there = hop
        key = (part, offset, axis, step)
        ids.setdefault(key, len(ids))
        target = side[axis] if axis != "z" else (z + step, seq)
        return pltpu.make_async_remote_copy(
            src_ref=block(part, offset), dst_ref=block(part, offset),
            send_sem=block_send.at[ids[key]], recv_sem=block_recv.at[recv_index(part, there)],
            device_id=target, device_id_type=MESH)

    def guarded(offset, hop, action):
        conds = []
        if offset[2]:
            conds.append(inside(offset[2]))
        if hop[0] == "z":
            conds.append(inside(hop[1]))
        if conds:
            pl.when(functools.reduce(lambda a, b: a & b, conds))(action)
        else:
            action()

    def start(part, offset, hop):
        guarded(offset, hop, lambda: send(part, offset, hop).start())
        pending.append((part, offset, hop))

    opening = [(part, hop) for part in range(3) for hop in forwards(ORDERS[part], (0, 0, 0), depth)]
    opening.sort(key=lambda item: ORDERS[item[0]].index(item[1][0]))
    for part, hop in opening:
        start(part, (0, 0, 0), hop)
    tok_send.start()
    tok_copy.start()
    others = []
    for step in range(1, n_seq):
        others.append(pltpu.make_async_remote_copy(
            src_ref=meta_ref, dst_ref=meta_all.at[seq], send_sem=meta_send.at[step],
            recv_sem=meta_recv.at[step], device_id=(z, lax.rem(seq + step, n_seq)),
            device_id_type=MESH))
        others[-1].start()

    def consume(part, offset, initial=False):
        begin, width = part_bounds(half)[part]
        chip = chip_of(offset)
        depth_cols = pl.ds(pl.multiple_of(chip * block_rows, block_rows), block_rows)
        tile = out_ref.shape[0] // 3

        @pl.loop(0, 3)
        def _(index):
            at = pl.ds(pl.multiple_of(index * tile, tile), tile)
            product = jnp.dot(tok_all[at, depth_cols], w_all[chip, :, pl.ds(begin, width)],
                              preferred_element_type=jnp.float32)
            if initial:
                out_ref[at, pl.ds(begin, width)] = product
            else:
                out_ref[at, pl.ds(begin, width)] += product

    def consume_guarded(part, offset):
        if offset[2]:
            pl.when(inside(offset[2]))(lambda: consume(part, offset))
        else:
            consume(part, offset)

    events = []
    for part in range(3):
        for dz in range(1 - depth, depth):
            for dy in range(2):
                for dx in range(2):
                    if (dx, dy, dz) != (0, 0, 0):
                        events.append((part, (dx, dy, dz)))

    def rank(event):
        part, offset = event
        hops = sum(abs(v) for v in offset)
        last = max(ORDERS[part].index(a) for a, v in zip("xyz", offset) if v)
        return (hops, last, part)

    events.sort(key=rank)
    lag = 6
    waiting = []
    ready = False

    def begin_products():
        tok_copy.wait()
        tok_send.wait()
        for part in range(3):
            consume(part, (0, 0, 0), initial=True)

    for part, offset in events:
        dz = offset[2]

        def arrive(part=part, offset=offset):
            own = block(part, offset)
            pltpu.make_async_remote_copy(
                src_ref=own, dst_ref=own, send_sem=block_send.at[0],
                recv_sem=block_recv.at[recv_index(part, offset)],
                device_id=partner, device_id_type=MESH).wait_recv()
        if dz:
            pl.when(inside(dz))(arrive)
        else:
            arrive()
        for hop in forwards(ORDERS[part], offset, depth):
            start(part, offset, hop)
        waiting.append((part, offset))
        if len(waiting) > lag:
            if not ready:
                begin_products()
                ready = True
            consume_guarded(*waiting.pop(0))
    if not ready:
        begin_products()
    for item in waiting:
        consume_guarded(*item)
    for copy in others:
        copy.wait()
    meta_all[seq] = meta_ref[...]
    meta_out[...] = meta_all[...]
    for part, offset, hop in pending:
        guarded(offset, hop, lambda: send(part, offset, hop).wait_send())


def count_sends(depth):
    total = 0
    for order in ORDERS:
        for dz in range(1 - depth, depth):
            for dy in range(2):
                for dx in range(2):
                    total += len(forwards(order, (dx, dy, dz), depth))
    return total


def project(token_rows, qkv_weight, meta):
    depth, n_seq = lax.axis_size("dp"), lax.axis_size("seq")
    rows, model = token_rows.shape
    columns = qkv_weight.shape[1]
    half = columns // CORES
    chips = depth * n_seq // CORES
    block_rows = model // chips
    sends = count_sends(depth)
    recvs = len(ORDERS) * (2 * depth - 1) * 4
    return pl.pallas_call(
        functools.partial(project_kernel, depth, n_seq),
        out_shape=(jax.ShapeDtypeStruct((CORES * rows, half), jnp.float32),
                   jax.ShapeDtypeStruct((n_seq,) + meta.shape, jnp.int32)),
        in_specs=[pl.BlockSpec(memory_space=pl.ANY), pl.BlockSpec(memory_space=pl.ANY),
                  pl.BlockSpec(memory_space=pltpu.VMEM)],
        out_specs=(pl.BlockSpec(memory_space=pltpu.VMEM), pl.BlockSpec(memory_space=pltpu.VMEM)),
        scratch_shapes=[
            pltpu.VMEM((CORES * rows, model), jnp.bfloat16),
            pltpu.VMEM((chips, block_rows, half), jnp.bfloat16),
            pltpu.VMEM((n_seq,) + meta.shape, jnp.int32),
            pltpu.SemaphoreType.DMA((4,)),
            pltpu.SemaphoreType.DMA((4,)),
            pltpu.SemaphoreType.DMA((4,)),
            pltpu.SemaphoreType.DMA((n_seq,)),
            pltpu.SemaphoreType.DMA((n_seq,)),
            pltpu.SemaphoreType.DMA((sends,)),
            pltpu.SemaphoreType.DMA((recvs,)),
        ],
        compiler_params=pltpu.CompilerParams(
            collective_id=0, has_side_effects=True, vmem_limit_bytes=44 * 2**20),
        cost_estimate=pl.CostEstimate(flops=2 * rows * model * columns,
                                      bytes_accessed=2 * model * columns, transcendentals=0),
    )(token_rows, qkv_weight, meta)


def project_plain(token_rows, qkv_weight, meta):
    n_seq = lax.axis_size("seq")
    core = lax.axis_index("seq") % CORES
    other = lax.ppermute(token_rows, "seq", [(i, i ^ 1) for i in range(n_seq)])
    pair = jnp.where(core == 0, jnp.concatenate([token_rows, other]),
                     jnp.concatenate([other, token_rows]))
    weight = lax.all_gather(qkv_weight, ("dp", "seq"), axis=0, tiled=True)
    heads_per = HEADS // CORES * HEAD_DIM
    kv_per = KV_HEADS // CORES * HEAD_DIM
    pieces = [
        lax.dynamic_slice_in_dim(weight, base + core * width, width, 1)
        for base, width in ((0, heads_per), (HEADS * HEAD_DIM, kv_per),
                            ((HEADS + KV_HEADS) * HEAD_DIM, kv_per))
    ]
    projected = jnp.dot(pair, jnp.concatenate(pieces, axis=1), preferred_element_type=jnp.float32)
    return projected, lax.all_gather(meta, "seq")


def positions(segment_ids, prefix_len):
    index_list = jnp.arange(segment_ids.shape[0], dtype=jnp.int32)
    fresh_doc = jnp.concatenate([jnp.ones((1,), jnp.bool_), segment_ids[1:] != segment_ids[:-1]])
    first_row = lax.cummax(jnp.where(fresh_doc, index_list, 0), axis=0)
    leading = segment_ids == segment_ids[0]
    return index_list - first_row + jnp.where(leading, prefix_len, 0)


def rotate(flat, position):
    rows, width = flat.shape
    heads = flat.reshape(rows, width // HEAD_DIM, HEAD_DIM)
    half_dim = HEAD_DIM // 2
    frequency = ROPE_BASE ** (-2.0 * jnp.arange(half_dim, dtype=jnp.float32) / HEAD_DIM)
    angles = position.astype(jnp.float32)[:, None] * frequency[None, :]
    cosine = jnp.cos(angles)[:, None, :]
    sine = jnp.sin(angles)[:, None, :]
    a, b = heads[..., :half_dim], heads[..., half_dim:]
    turned = jnp.concatenate([a * cosine - b * sine, b * cosine + a * sine], axis=-1)
    return turned.reshape(rows, width).astype(jnp.bfloat16)


def attend_kernel(tile, reach_ref, prefix_ref, q_ref, k_ref, v_ref, col_ref, row_ref, out_ref):
    block = pl.program_id(0)
    count = q_ref.shape[1]
    group = q_ref.shape[2] // HEAD_DIM
    prefix = prefix_ref[block]
    factor = HEAD_DIM ** -0.5 * 1.4426950408889634

    def run(index, remote):
        at = pl.ds(pl.multiple_of(index * tile, tile), tile)
        blocks = remote + 1
        window = pl.ds(block + REACH - remote, blocks)
        keys = k_ref[window].reshape(blocks * count, HEAD_DIM)
        values = v_ref[window].reshape(blocks * count, HEAD_DIM)
        ids = col_ref[0, at, :]
        columns = lax.broadcasted_iota(jnp.int32, (tile, count), 1)
        lines = lax.broadcasted_iota(jnp.int32, (tile, count), 0) + index * tile
        seen = (columns <= lines) & (row_ref[0] == ids)
        if remote:
            back = lax.broadcasted_iota(jnp.int32, (tile, remote * count), 1) - remote * count
            lead = ids == row_ref[0][:, :1]
            seen = jnp.concatenate([(back >= -prefix) & lead, seen], axis=1)
        for head in range(group):
            cols = pl.ds(head * HEAD_DIM, HEAD_DIM)
            scores = lax.dot_general(q_ref[0, at, cols], keys, (((1,), (1,)), ((), ())),
                                     preferred_element_type=jnp.float32)
            scores = jnp.where(seen, scores, MASKED)
            top = jnp.max(scores, axis=-1, keepdims=True)
            expo = jnp.exp2((scores - top) * factor)
            total = jnp.sum(expo, axis=-1, keepdims=True)
            probs = (expo * (1.0 / total)).astype(jnp.bfloat16)
            out_ref[0, at, cols] = jnp.dot(
                probs, values, preferred_element_type=jnp.float32).astype(jnp.bfloat16)

    @pl.loop(0, count // tile)
    def _(index):
        remote = reach_ref[block, index]
        for blocks in range(REACH + 1):
            low = remote > (blocks - 1) * count
            high = remote <= blocks * count
            cond = low & high if 0 < blocks < REACH else (high if blocks == 0 else low)
            pl.when(cond)(functools.partial(run, index, blocks))


def attend(queries, keys, values, segs, prefix):
    blocks, count, width = queries.shape
    kv_heads = keys.shape[2] // HEAD_DIM
    group = width // kv_heads
    tile = 128
    starts = segs[:, ::tile]
    reach = jnp.where(starts == segs[:, :1], prefix[:, None], 0)
    smem = pl.BlockSpec(memory_space=pltpu.SMEM)
    return pl.pallas_call(
        functools.partial(attend_kernel, tile),
        grid=(blocks, kv_heads),
        out_shape=jax.ShapeDtypeStruct(queries.shape, jnp.bfloat16),
        in_specs=[
            smem, smem,
            pl.BlockSpec((1, count, group), lambda b, h: (b, 0, h)),
            pl.BlockSpec((keys.shape[0], count, HEAD_DIM), lambda b, h: (0, 0, h)),
            pl.BlockSpec((keys.shape[0], count, HEAD_DIM), lambda b, h: (0, 0, h)),
            pl.BlockSpec((1, count, 1), lambda b, h: (b, 0, 0)),
            pl.BlockSpec((1, 1, count), lambda b, h: (b, 0, 0)),
        ],
        out_specs=pl.BlockSpec((1, count, group), lambda b, h: (b, 0, h)),
        compiler_params=pltpu.CompilerParams(vmem_limit_bytes=32 * 2**20),
        cost_estimate=pl.CostEstimate(
            flops=4 * blocks * count * width * count * (REACH + 1),
            bytes_accessed=8 * blocks * count * width, transcendentals=0),
    )(reach, prefix, queries, keys, values, segs[:, :, None], segs[:, None, :])


def on_device(tokens, qkv_weight, segments, destination, doc_prefix):
    n_seq = lax.axis_size("seq")
    me = lax.axis_index("seq")
    count = tokens.shape[1]
    meta = jnp.zeros((META_ROWS, count), jnp.int32)
    meta = meta.at[0].set(segments[0]).at[1].set(destination[0]).at[2].set(doc_prefix[0, 0])
    planar = n_seq == 4 * CORES
    projected, metas = (project if planar else project_plain)(tokens[0], qkv_weight, meta)

    pair = lax.dynamic_slice_in_dim(metas, me // CORES * CORES, CORES, 0)
    segs, prefix = pair[:, 0], pair[:, 2, 0]
    targets = pair[:, 1]
    heads_per = HEADS // CORES * HEAD_DIM
    kv_per = KV_HEADS // CORES * HEAD_DIM
    position = jax.vmap(positions)(segs, prefix).reshape(-1)
    keys = rotate(projected[:, heads_per : heads_per + kv_per], position)
    values = projected[:, heads_per + kv_per :].astype(jnp.bfloat16)
    own = jnp.concatenate([keys, values], axis=1)
    before = lax.ppermute(own, "seq", [(i, i + CORES) for i in range(n_seq - CORES)])
    queries = rotate(projected[:, :heads_per], position).reshape(CORES, count, heads_per)
    span = jnp.concatenate([before, own]).reshape(2 * CORES, count, 2 * kv_per)
    heads_out = attend(queries, span[:, :, :kv_per], span[:, :, kv_per:], segs, prefix)

    capacity = count // min(n_seq, 16)
    slots = jnp.arange(n_seq * capacity, dtype=jnp.int32)

    def pick(target, rows):
        owner = target // count
        one_hot = (owner[:, None] == jnp.arange(n_seq, dtype=jnp.int32)[None, :]).astype(jnp.int32)
        order = jnp.sum(jnp.cumsum(one_hot, axis=0) * one_hot, axis=1) - 1
        chosen = (slots[:, None] == (owner * capacity + order)[None, :]).astype(jnp.bfloat16)
        return jnp.dot(chosen, rows, preferred_element_type=jnp.float32).astype(jnp.bfloat16)

    send_rows = jnp.stack(
        [pick(targets[j], heads_out[j]).reshape(n_seq, capacity, heads_per) for j in range(CORES)],
        axis=1)
    got = lax.all_to_all(send_rows, "seq", split_axis=0, concat_axis=0, tiled=True)
    got = got.reshape(n_seq // CORES, CORES, CORES, capacity, heads_per)

    everyone = metas[:, 1]
    ours = everyone // count == me
    order = jnp.cumsum(ours.astype(jnp.int32), axis=1) - 1
    match = ours[:, None, :] & (
        order[:, None, :] == jnp.arange(capacity, dtype=jnp.int32)[None, :, None])
    places = jnp.sum(jnp.where(match, everyone[:, None, :] % count + 1, 0), axis=2) - 1
    put = (jnp.arange(count, dtype=jnp.int32)[:, None] == places.reshape(1, -1)).astype(jnp.bfloat16)
    halves = [
        jnp.dot(put, got[:, c].reshape(n_seq * capacity, heads_per),
                preferred_element_type=jnp.float32).astype(jnp.bfloat16)
        for c in range(CORES)
    ]
    return jnp.concatenate(halves, axis=1)[None]


def solution(mesh):
    placed = (
        P("dp", "seq", None),
        P(("dp", "seq"), None),
        P("dp", "seq"),
        P("dp", "seq"),
        P("dp", "seq"),
    )
    return jax.shard_map(
        on_device, mesh=mesh, in_specs=placed, out_specs=P("dp", "seq", None), check_vma=False
    )
```

```python
import functools

import jax
import jax.numpy as jnp
from jax import lax
from jax.experimental import pallas as pl
from jax.experimental.pallas import tpu as pltpu
from jax.sharding import PartitionSpec as P

HEADS = 16
KV_HEADS = 4
HEAD_DIM = 128
REACH = 2
ROPE_BASE = 500000.0
MASKED = -1e30
CORES = 2
MESH = pl.DeviceIdType.MESH
META_ROWS = 8

ORDERS = ("zxy", "zyx", "xyz")
HEAD_START = (2.5, 0, 0)


def part_bounds(width):
    unit = width // 12
    return ((0, 4 * unit), (4 * unit, 5 * unit), (9 * unit, 3 * unit))


def forwards(order, offset, depth):
    delta = dict(zip("xyz", offset))
    last = max([order.index(a) for a in order if delta[a]], default=-1)
    hops = []
    for index, axis in enumerate(order):
        if index < last:
            continue
        if axis == "z":
            steps = (1, -1) if delta["z"] == 0 else ((1,) if delta["z"] < 0 else (-1,))
            for step in steps:
                if abs(delta["z"] - step) < depth:
                    hops.append(("z", step, (delta["x"], delta["y"], delta["z"] - step)))
        elif index > last:
            there = dict(delta)
            there[axis] = 1
            hops.append((axis, 1, (there["x"], there["y"], there["z"])))
    return hops


def project_kernel(depth, n_seq, tok_ref, w_ref, meta_ref, turn_ref, query_out, kv_out, meta_out,
                   tok_all, w_all, meta_all, turn_all, total, kv_before, local_sem, pair_send,
                   pair_recv, meta_send, meta_recv, block_send, block_recv, kv_send, kv_recv):
    z = lax.axis_index("dp")
    seq = lax.axis_index("seq")
    core = lax.rem(seq, CORES)
    plane = seq // CORES
    x = lax.rem(plane, 2)
    y = plane // 2
    rows, model = tok_ref.shape
    shard = w_ref.shape[0]
    half = total.shape[1]
    planes = n_seq // CORES
    heads_per = HEADS // CORES * HEAD_DIM
    kv_per = KV_HEADS // CORES * HEAD_DIM
    block_rows = shard * CORES
    partner = (z, seq + 1 - 2 * core)
    side = {
        "x": (z, (y * 2 + 1 - x) * CORES + core),
        "y": (z, ((1 - y) * 2 + x) * CORES + core),
    }
    follower = (z, lax.rem(seq + CORES, n_seq))

    def inside(dz):
        return (z + dz >= 0) & (z + dz < depth)

    barrier = pltpu.get_barrier_semaphore()
    for step in range(1, n_seq):
        pl.semaphore_signal(barrier, inc=1, device_id=(z, lax.rem(seq + step, n_seq)),
                            device_id_type=MESH)
    for step in (1, -1):
        @pl.when(inside(step))
        def _(step=step):
            pl.semaphore_signal(barrier, inc=1, device_id=(z + step, seq), device_id_type=MESH)
    peers = n_seq - 1 + jnp.where(z > 0, 1, 0) + jnp.where(z < depth - 1, 1, 0)
    pl.semaphore_wait(barrier, peers)

    def chip_of(offset):
        dx, dy, dz = offset
        cx = 1 - x if dx else x
        cy = 1 - y if dy else y
        return ((z + dz) * 2 + cy) * 2 + cx

    mine = chip_of((0, 0, 0))
    own_rows = pl.ds(pl.multiple_of(core * shard, shard), shard)
    slices = ((HEADS * HEAD_DIM, 0, kv_per),
              ((HEADS + KV_HEADS) * HEAD_DIM, kv_per, kv_per),
              (0, 2 * kv_per, heads_per))
    first = []
    for index, (base, place, width) in enumerate(slices):
        there = pl.ds(pl.multiple_of(base + (1 - core) * width, 128), width)
        here = pl.ds(pl.multiple_of(base + core * width, 128), width)
        first.append(pltpu.make_async_remote_copy(
            src_ref=w_ref.at[:, there], dst_ref=w_all.at[mine, own_rows, pl.ds(place, width)],
            send_sem=pair_send.at[index], recv_sem=pair_recv.at[index],
            device_id=partner, device_id_type=MESH))
        first.append(pltpu.make_async_copy(
            w_ref.at[:, here], w_all.at[mine, own_rows, pl.ds(place, width)],
            local_sem.at[index]))
    for copy in first:
        copy.start()
    tok_rows = pl.ds(pl.multiple_of(core * rows, rows), rows)
    tok_send = pltpu.make_async_remote_copy(
        src_ref=tok_ref, dst_ref=tok_all.at[tok_rows, :], send_sem=pair_send.at[3],
        recv_sem=pair_recv.at[3], device_id=partner, device_id_type=MESH)
    tok_copy = pltpu.make_async_copy(tok_ref, tok_all.at[tok_rows, :], local_sem.at[3])
    turn_send = pltpu.make_async_remote_copy(
        src_ref=turn_ref, dst_ref=turn_all.at[tok_rows, :], send_sem=pair_send.at[4],
        recv_sem=pair_recv.at[4], device_id=partner, device_id_type=MESH)
    turn_copy = pltpu.make_async_copy(turn_ref, turn_all.at[tok_rows, :], local_sem.at[4])
    for copy in first:
        copy.wait()

    ids = {}
    pending = []

    def block(part, offset):
        start, width = part_bounds(half)[part]
        return w_all.at[chip_of(offset), :, pl.ds(start, width)]

    def recv_index(part, offset):
        dx, dy, dz = offset
        return ((part * (2 * depth - 1) + dz + depth - 1) * 2 + dy) * 2 + dx

    def send(part, offset, hop):
        axis, step, there = hop
        key = (part, offset, axis, step)
        ids.setdefault(key, len(ids))
        target = side[axis] if axis != "z" else (z + step, seq)
        return pltpu.make_async_remote_copy(
            src_ref=block(part, offset), dst_ref=block(part, offset),
            send_sem=block_send.at[ids[key]], recv_sem=block_recv.at[recv_index(part, there)],
            device_id=target, device_id_type=MESH)

    def guarded(offset, hop, action):
        conds = []
        if offset[2]:
            conds.append(inside(offset[2]))
        if hop[0] == "z":
            conds.append(inside(hop[1]))
        if conds:
            pl.when(functools.reduce(lambda a, b: a & b, conds))(action)
        else:
            action()

    def start(part, offset, hop):
        guarded(offset, hop, lambda: send(part, offset, hop).start())
        pending.append((part, offset, hop))

    opening = [(part, hop) for part in range(3) for hop in forwards(ORDERS[part], (0, 0, 0), depth)]
    opening.sort(key=lambda item: ORDERS[item[0]].index(item[1][0]))
    for part, hop in opening:
        start(part, (0, 0, 0), hop)
    tok_send.start()
    tok_copy.start()
    turn_send.start()
    turn_copy.start()
    others = []
    for step in range(1, n_seq):
        others.append(pltpu.make_async_remote_copy(
            src_ref=meta_ref, dst_ref=meta_all.at[seq], send_sem=meta_send.at[step],
            recv_sem=meta_recv.at[step], device_id=(z, lax.rem(seq + step, n_seq)),
            device_id_type=MESH))
        others[-1].start()

    def consume(part, offset, initial=False):
        begin, width = part_bounds(half)[part]
        chip = chip_of(offset)
        depth_cols = pl.ds(pl.multiple_of(chip * block_rows, block_rows), block_rows)
        tile = total.shape[0] // 3

        @pl.loop(0, 3)
        def _(index):
            at = pl.ds(pl.multiple_of(index * tile, tile), tile)
            product = jnp.dot(tok_all[at, depth_cols], w_all[chip, :, pl.ds(begin, width)],
                              preferred_element_type=jnp.float32)
            if initial:
                total[at, pl.ds(begin, width)] = product
            else:
                total[at, pl.ds(begin, width)] += product

    def consume_guarded(part, offset):
        if offset[2]:
            pl.when(inside(offset[2]))(lambda: consume(part, offset))
        else:
            consume(part, offset)

    events = []
    for part in range(3):
        for dz in range(1 - depth, depth):
            for dy in range(2):
                for dx in range(2):
                    if (dx, dy, dz) != (0, 0, 0):
                        events.append((part, (dx, dy, dz)))

    def rank(event):
        part, offset = event
        hops = sum(abs(v) for v in offset)
        last = max(ORDERS[part].index(a) for a, v in zip("xyz", offset) if v)
        return (hops - HEAD_START[part], last, part)

    events.sort(key=rank)
    lag = 6
    waiting = []
    ready = False

    def begin_products():
        tok_copy.wait()
        tok_send.wait()
        turn_copy.wait()
        turn_send.wait()
        for part in range(3):
            consume(part, (0, 0, 0), initial=True)

    def turned(at, begin):
        heads = total[at, pl.ds(begin, HEAD_DIM)]
        swapped = pltpu.roll(heads, HEAD_DIM // 2, 1)
        angle = turn_all[at, :]
        return (heads * angle[:, :HEAD_DIM] + swapped * angle[:, HEAD_DIM:]).astype(jnp.bfloat16)

    kv_copy = pltpu.make_async_remote_copy(
        src_ref=kv_out.at[pl.ds(CORES, CORES)], dst_ref=kv_before, send_sem=kv_send,
        recv_sem=kv_recv, device_id=follower, device_id_type=MESH)

    def share_kv():
        for index in range(CORES):
            at = pl.ds(index * rows, rows)
            for begin in range(0, kv_per, HEAD_DIM):
                kv_out[CORES + index, :, pl.ds(begin, HEAD_DIM)] = turned(at, begin)
            kv_out[CORES + index, :, pl.ds(kv_per, kv_per)] = total[
                at, pl.ds(kv_per, kv_per)].astype(jnp.bfloat16)
        pl.when(plane < planes - 1)(lambda: kv_copy.start())

    def use(item):
        consume_guarded(*item)
        left[item[0]] -= 1
        if item[0] == 0 and left[0] == 0:
            share_kv()

    left = [sum(1 for event in events if event[0] == part) for part in range(3)]
    for part, offset in events:
        dz = offset[2]

        def arrive(part=part, offset=offset):
            own = block(part, offset)
            pltpu.make_async_remote_copy(
                src_ref=own, dst_ref=own, send_sem=block_send.at[0],
                recv_sem=block_recv.at[recv_index(part, offset)],
                device_id=partner, device_id_type=MESH).wait_recv()
        if dz:
            pl.when(inside(dz))(arrive)
        else:
            arrive()
        for hop in forwards(ORDERS[part], offset, depth):
            start(part, offset, hop)
        waiting.append((part, offset))
        if len(waiting) > lag:
            if not ready:
                begin_products()
                ready = True
            use(waiting.pop(0))
    if not ready:
        begin_products()
    for item in waiting:
        use(item)
    for index in range(CORES):
        at = pl.ds(index * rows, rows)
        for begin in range(0, heads_per, HEAD_DIM):
            query_out[index, :, pl.ds(begin, HEAD_DIM)] = turned(at, 2 * kv_per + begin)
    for copy in others:
        copy.wait()
    meta_all[seq] = meta_ref[...]
    meta_out[...] = meta_all[...]

    @pl.when(plane > 0)
    def _():
        kv_copy.wait_recv()
        kv_out[0:CORES] = kv_before[...]

    @pl.when(plane == 0)
    def _():
        kv_out[0:CORES] = jnp.zeros_like(kv_before)

    pl.when(plane < planes - 1)(lambda: kv_copy.wait_send())
    for part, offset, hop in pending:
        guarded(offset, hop, lambda: send(part, offset, hop).wait_send())


def count_sends(depth):
    total = 0
    for order in ORDERS:
        for dz in range(1 - depth, depth):
            for dy in range(2):
                for dx in range(2):
                    total += len(forwards(order, (dx, dy, dz), depth))
    return total


def project(token_rows, qkv_weight, meta, turn):
    depth, n_seq = lax.axis_size("dp"), lax.axis_size("seq")
    rows, model = token_rows.shape
    columns = qkv_weight.shape[1]
    half = columns // CORES
    queries = HEADS // CORES * HEAD_DIM
    kv_width = half - queries
    chips = depth * n_seq // CORES
    block_rows = model // chips
    sends = count_sends(depth)
    recvs = len(ORDERS) * (2 * depth - 1) * 4
    vmem = pl.BlockSpec(memory_space=pltpu.VMEM)
    return pl.pallas_call(
        functools.partial(project_kernel, depth, n_seq),
        out_shape=(jax.ShapeDtypeStruct((CORES, rows, queries), jnp.bfloat16),
                   jax.ShapeDtypeStruct((2 * CORES, rows, kv_width), jnp.bfloat16),
                   jax.ShapeDtypeStruct((n_seq,) + meta.shape, jnp.int32)),
        in_specs=[pl.BlockSpec(memory_space=pl.ANY), pl.BlockSpec(memory_space=pl.ANY),
                  vmem, vmem],
        out_specs=(vmem, vmem, vmem),
        scratch_shapes=[
            pltpu.VMEM((CORES * rows, model), jnp.bfloat16),
            pltpu.VMEM((chips, block_rows, half), jnp.bfloat16),
            pltpu.VMEM((n_seq,) + meta.shape, jnp.int32),
            pltpu.VMEM((CORES * rows, 2 * HEAD_DIM), jnp.float32),
            pltpu.VMEM((CORES * rows, half), jnp.float32),
            pltpu.VMEM((CORES, rows, kv_width), jnp.bfloat16),
            pltpu.SemaphoreType.DMA((5,)),
            pltpu.SemaphoreType.DMA((5,)),
            pltpu.SemaphoreType.DMA((5,)),
            pltpu.SemaphoreType.DMA((n_seq,)),
            pltpu.SemaphoreType.DMA((n_seq,)),
            pltpu.SemaphoreType.DMA((sends,)),
            pltpu.SemaphoreType.DMA((recvs,)),
            pltpu.SemaphoreType.DMA,
            pltpu.SemaphoreType.DMA,
        ],
        compiler_params=pltpu.CompilerParams(
            collective_id=0, has_side_effects=True, vmem_limit_bytes=60 * 2**20),
        cost_estimate=pl.CostEstimate(flops=2 * rows * model * columns,
                                      bytes_accessed=2 * model * columns, transcendentals=0),
    )(token_rows, qkv_weight, meta, turn)


def project_plain(token_rows, qkv_weight, meta, turn):
    n_seq = lax.axis_size("seq")
    rows = token_rows.shape[0]
    core = lax.axis_index("seq") % CORES

    def paired(block):
        other = lax.ppermute(block, "seq", [(i, i ^ 1) for i in range(n_seq)])
        return jnp.where(core == 0, jnp.concatenate([block, other]),
                         jnp.concatenate([other, block]))

    weight = lax.all_gather(qkv_weight, ("dp", "seq"), axis=0, tiled=True)
    heads_per = HEADS // CORES * HEAD_DIM
    kv_per = KV_HEADS // CORES * HEAD_DIM
    pieces = [
        lax.dynamic_slice_in_dim(weight, base + core * width, width, 1)
        for base, width in ((0, heads_per), (HEADS * HEAD_DIM, kv_per),
                            ((HEADS + KV_HEADS) * HEAD_DIM, kv_per))
    ]
    projected = jnp.dot(paired(token_rows), jnp.concatenate(pieces, axis=1),
                        preferred_element_type=jnp.float32)
    angle = paired(turn)

    def turned(flat):
        heads = flat.reshape(flat.shape[0], -1, HEAD_DIM)
        swapped = jnp.roll(heads, HEAD_DIM // 2, axis=2)
        both = heads * angle[:, None, :HEAD_DIM] + swapped * angle[:, None, HEAD_DIM:]
        return both.reshape(flat.shape).astype(jnp.bfloat16)

    queries = turned(projected[:, :heads_per]).reshape(CORES, rows, heads_per)
    keys = turned(projected[:, heads_per : heads_per + kv_per])
    values = projected[:, heads_per + kv_per :].astype(jnp.bfloat16)
    own = jnp.concatenate([keys, values], axis=1)
    before = lax.ppermute(own, "seq", [(i, i + CORES) for i in range(n_seq - CORES)])
    span = jnp.concatenate([before, own]).reshape(2 * CORES, rows, 2 * kv_per)
    return queries, span, lax.all_gather(meta, "seq")


def turns(segment_ids, prefix_len):
    first_row = jnp.sum(
        (segment_ids[None, :] < segment_ids[:, None]).astype(jnp.int32), axis=1)
    index_list = jnp.arange(segment_ids.shape[0], dtype=jnp.int32)
    leading = segment_ids == segment_ids[0]
    position = index_list - first_row + jnp.where(leading, prefix_len, 0)
    half_dim = HEAD_DIM // 2
    frequency = ROPE_BASE ** (-2.0 * jnp.arange(half_dim, dtype=jnp.float32) / HEAD_DIM)
    angles = position.astype(jnp.float32)[:, None] * frequency[None, :]
    cosine, sine = jnp.cos(angles), jnp.sin(angles)
    return jnp.concatenate([cosine, cosine, -sine, sine], axis=1)


def attend_kernel(tile, reach_ref, prefix_ref, q_ref, k_ref, v_ref, col_ref, row_ref, out_ref):
    block = pl.program_id(0)
    count = q_ref.shape[1]
    group = q_ref.shape[2] // HEAD_DIM
    prefix = prefix_ref[block]
    factor = HEAD_DIM ** -0.5 * 1.4426950408889634

    def run(index, remote):
        at = pl.ds(pl.multiple_of(index * tile, tile), tile)
        blocks = remote + 1
        window = pl.ds(block + REACH - remote, blocks)
        keys = k_ref[window].reshape(blocks * count, HEAD_DIM)
        values = v_ref[window].reshape(blocks * count, HEAD_DIM)
        ids = col_ref[0, at, :]
        columns = lax.broadcasted_iota(jnp.int32, (tile, count), 1)
        lines = lax.broadcasted_iota(jnp.int32, (tile, count), 0) + index * tile
        seen = (columns <= lines) & (row_ref[0] == ids)
        if remote:
            back = lax.broadcasted_iota(jnp.int32, (tile, remote * count), 1) - remote * count
            lead = ids == row_ref[0][:, :1]
            seen = jnp.concatenate([(back >= -prefix) & lead, seen], axis=1)
        parts = [pl.ds(head * HEAD_DIM, HEAD_DIM) for head in range(group)]
        queries = jnp.concatenate([q_ref[0, at, cols] for cols in parts], axis=0)
        scores = lax.dot_general(queries, keys, (((1,), (1,)), ((), ())),
                                 preferred_element_type=jnp.float32)
        scores = scores.reshape(group, tile, blocks * count)
        scores = jnp.where(seen[None], scores, MASKED)
        top = jnp.max(scores, axis=-1, keepdims=True)
        expo = jnp.exp2((scores - top) * factor)
        total = jnp.sum(expo, axis=-1, keepdims=True)
        probs = (expo * (1.0 / total)).astype(jnp.bfloat16)
        out = jnp.dot(probs.reshape(group * tile, blocks * count), values,
                      preferred_element_type=jnp.float32).astype(jnp.bfloat16)
        for head, cols in enumerate(parts):
            out_ref[0, at, cols] = out[head * tile : (head + 1) * tile]

    @pl.loop(0, count // tile)
    def _(index):
        remote = reach_ref[block, index]
        for blocks in range(REACH + 1):
            low = remote > (blocks - 1) * count
            high = remote <= blocks * count
            cond = low & high if 0 < blocks < REACH else (high if blocks == 0 else low)
            pl.when(cond)(functools.partial(run, index, blocks))


def attend(queries, span, segs, prefix):
    blocks, count, width = queries.shape
    kv_heads = span.shape[2] // HEAD_DIM // 2
    group = width // kv_heads
    tile = 128
    starts = segs[:, ::tile]
    reach = jnp.where(starts == segs[:, :1], prefix[:, None], 0)
    smem = pl.BlockSpec(memory_space=pltpu.SMEM)
    return pl.pallas_call(
        functools.partial(attend_kernel, tile),
        grid=(blocks, kv_heads),
        out_shape=jax.ShapeDtypeStruct(queries.shape, jnp.bfloat16),
        in_specs=[
            smem, smem,
            pl.BlockSpec((1, count, group), lambda b, h: (b, 0, h)),
            pl.BlockSpec((span.shape[0], count, HEAD_DIM), lambda b, h: (0, 0, h)),
            pl.BlockSpec((span.shape[0], count, HEAD_DIM), lambda b, h: (0, 0, kv_heads + h)),
            pl.BlockSpec((1, count, 1), lambda b, h: (b, 0, 0)),
            pl.BlockSpec((1, 1, count), lambda b, h: (b, 0, 0)),
        ],
        out_specs=pl.BlockSpec((1, count, group), lambda b, h: (b, 0, h)),
        compiler_params=pltpu.CompilerParams(vmem_limit_bytes=32 * 2**20),
        cost_estimate=pl.CostEstimate(
            flops=4 * blocks * count * width * count * (REACH + 1),
            bytes_accessed=8 * blocks * count * width, transcendentals=0),
    )(reach, prefix, queries, span, span, segs[:, :, None], segs[:, None, :])


def on_device(tokens, qkv_weight, segments, destination, doc_prefix):
    n_seq = lax.axis_size("seq")
    me = lax.axis_index("seq")
    count = tokens.shape[1]
    prefix_row = jnp.broadcast_to(doc_prefix[0], (count,))
    meta = jnp.stack([segments[0], destination[0]] + [prefix_row] * (META_ROWS - 2))
    turn = turns(segments[0], doc_prefix[0, 0])
    planar = n_seq == 4 * CORES
    queries, span, metas = (project if planar else project_plain)(
        tokens[0], qkv_weight, meta, turn)

    pair = lax.dynamic_slice_in_dim(metas, me // CORES * CORES, CORES, 0)
    segs, targets, prefix = pair[:, 0], pair[:, 1], pair[:, 2, 0]
    heads_per = queries.shape[2]
    heads_out = attend(queries, span, segs, prefix)

    capacity = count // min(n_seq, 16)
    slots = jnp.arange(n_seq * capacity, dtype=jnp.int32)

    def pick(target, rows):
        owner = target // count
        one_hot = (owner[:, None] == jnp.arange(n_seq, dtype=jnp.int32)[None, :]).astype(jnp.int32)
        order = jnp.sum(jnp.cumsum(one_hot, axis=0) * one_hot, axis=1) - 1
        chosen = (slots[:, None] == (owner * capacity + order)[None, :]).astype(jnp.bfloat16)
        return jnp.dot(chosen, rows, preferred_element_type=jnp.float32).astype(jnp.bfloat16)

    send_rows = jnp.stack(
        [pick(targets[j], heads_out[j]).reshape(n_seq, capacity, heads_per) for j in range(CORES)],
        axis=1)
    got = lax.all_to_all(send_rows, "seq", split_axis=0, concat_axis=0, tiled=True)
    got = got.reshape(n_seq // CORES, CORES, CORES, capacity, heads_per)

    everyone = metas[:, 1]
    ours = everyone // count == me
    order = jnp.cumsum(ours.astype(jnp.int32), axis=1) - 1
    match = ours[:, None, :] & (
        order[:, None, :] == jnp.arange(capacity, dtype=jnp.int32)[None, :, None])
    places = jnp.sum(jnp.where(match, everyone[:, None, :] % count + 1, 0), axis=2) - 1
    put = (jnp.arange(count, dtype=jnp.int32)[:, None] == places.reshape(1, -1)).astype(jnp.bfloat16)
    halves = [
        jnp.dot(put, got[:, c].reshape(n_seq * capacity, heads_per),
                preferred_element_type=jnp.float32).astype(jnp.bfloat16)
        for c in range(CORES)
    ]
    return jnp.concatenate(halves, axis=1)[None]


def solution(mesh):
    placed = (
        P("dp", "seq", None),
        P(("dp", "seq"), None),
        P("dp", "seq"),
        P("dp", "seq"),
        P("dp", "seq"),
    )
    return jax.shard_map(
        on_device, mesh=mesh, in_specs=placed, out_specs=P("dp", "seq", None), check_vma=False
    )
```

```python
import functools

import jax
import jax.numpy as jnp
from jax import lax
from jax.experimental import pallas as pl
from jax.experimental.pallas import tpu as pltpu
from jax.sharding import PartitionSpec as P

HEADS = 16
KV_HEADS = 4
HEAD_DIM = 128
REACH = 2
ROPE_BASE = 500000.0
MASKED = -1e30
CORES = 2
MESH = pl.DeviceIdType.MESH
META_ROWS = 8

ORDERS = ("zxy", "zyx", "xyz")
BASES = (-1.5, -2.0, -2.5)
HOP_COSTS = ((4.25, 3.75, 0.75), (4.75, 4.25, 0.75), (3.75, 2.25, 3.0))
OPENING = ((8.0, -5.5, 6.0), (4.0, 2.0, -11.0), (-1.5, 0.0, 11.5))


def part_bounds(width):
    unit = width // 12
    return ((0, 4 * unit), (4 * unit, 5 * unit), (9 * unit, 3 * unit))


def forwards(order, offset, depth):
    delta = dict(zip("xyz", offset))
    last = max([order.index(a) for a in order if delta[a]], default=-1)
    hops = []
    for index, axis in enumerate(order):
        if index < last:
            continue
        if axis == "z":
            steps = (1, -1) if delta["z"] == 0 else ((1,) if delta["z"] < 0 else (-1,))
            for step in steps:
                if abs(delta["z"] - step) < depth:
                    hops.append(("z", step, (delta["x"], delta["y"], delta["z"] - step)))
        elif index > last:
            there = dict(delta)
            there[axis] = 1
            hops.append((axis, 1, (there["x"], there["y"], there["z"])))
    return hops


def project_kernel(depth, n_seq, tok_ref, w_ref, meta_ref, turn_ref, query_out, kv_out, meta_out,
                   tok_all, w_all, meta_all, turn_all, total, kv_before, local_sem, pair_send,
                   pair_recv, meta_send, meta_recv, block_send, block_recv, kv_send, kv_recv):
    z = lax.axis_index("dp")
    seq = lax.axis_index("seq")
    core = lax.rem(seq, CORES)
    plane = seq // CORES
    x = lax.rem(plane, 2)
    y = plane // 2
    rows, model = tok_ref.shape
    shard = w_ref.shape[0]
    half = total.shape[1]
    planes = n_seq // CORES
    heads_per = HEADS // CORES * HEAD_DIM
    kv_per = KV_HEADS // CORES * HEAD_DIM
    block_rows = shard * CORES
    partner = (z, seq + 1 - 2 * core)
    side = {
        "x": (z, (y * 2 + 1 - x) * CORES + core),
        "y": (z, ((1 - y) * 2 + x) * CORES + core),
    }
    follower = (z, lax.rem(seq + CORES, n_seq))

    def inside(dz):
        return (z + dz >= 0) & (z + dz < depth)

    barrier = pltpu.get_barrier_semaphore()
    for step in range(1, n_seq):
        pl.semaphore_signal(barrier, inc=1, device_id=(z, lax.rem(seq + step, n_seq)),
                            device_id_type=MESH)
    for step in (1, -1):
        @pl.when(inside(step))
        def _(step=step):
            pl.semaphore_signal(barrier, inc=1, device_id=(z + step, seq), device_id_type=MESH)
    peers = n_seq - 1 + jnp.where(z > 0, 1, 0) + jnp.where(z < depth - 1, 1, 0)
    pl.semaphore_wait(barrier, peers)

    def chip_of(offset):
        dx, dy, dz = offset
        cx = 1 - x if dx else x
        cy = 1 - y if dy else y
        return ((z + dz) * 2 + cy) * 2 + cx

    mine = chip_of((0, 0, 0))
    own_rows = pl.ds(pl.multiple_of(core * shard, shard), shard)
    slices = ((HEADS * HEAD_DIM, 0, kv_per),
              ((HEADS + KV_HEADS) * HEAD_DIM, kv_per, kv_per),
              (0, 2 * kv_per, heads_per))
    first = []
    for index, (base, place, width) in enumerate(slices):
        there = pl.ds(pl.multiple_of(base + (1 - core) * width, 128), width)
        here = pl.ds(pl.multiple_of(base + core * width, 128), width)
        first.append(pltpu.make_async_remote_copy(
            src_ref=w_ref.at[:, there], dst_ref=w_all.at[mine, own_rows, pl.ds(place, width)],
            send_sem=pair_send.at[index], recv_sem=pair_recv.at[index],
            device_id=partner, device_id_type=MESH))
        first.append(pltpu.make_async_copy(
            w_ref.at[:, here], w_all.at[mine, own_rows, pl.ds(place, width)],
            local_sem.at[index]))
    for copy in first:
        copy.start()
    tok_rows = pl.ds(pl.multiple_of(core * rows, rows), rows)
    tok_send = pltpu.make_async_remote_copy(
        src_ref=tok_ref, dst_ref=tok_all.at[tok_rows, :], send_sem=pair_send.at[3],
        recv_sem=pair_recv.at[3], device_id=partner, device_id_type=MESH)
    tok_copy = pltpu.make_async_copy(tok_ref, tok_all.at[tok_rows, :], local_sem.at[3])
    turn_send = pltpu.make_async_remote_copy(
        src_ref=turn_ref, dst_ref=turn_all.at[tok_rows, :], send_sem=pair_send.at[4],
        recv_sem=pair_recv.at[4], device_id=partner, device_id_type=MESH)
    turn_copy = pltpu.make_async_copy(turn_ref, turn_all.at[tok_rows, :], local_sem.at[4])
    for copy in first:
        copy.wait()

    ids = {}
    pending = []

    def block(part, offset):
        start, width = part_bounds(half)[part]
        return w_all.at[chip_of(offset), :, pl.ds(start, width)]

    def recv_index(part, offset):
        dx, dy, dz = offset
        return ((part * (2 * depth - 1) + dz + depth - 1) * 2 + dy) * 2 + dx

    def send(part, offset, hop):
        axis, step, there = hop
        key = (part, offset, axis, step)
        ids.setdefault(key, len(ids))
        target = side[axis] if axis != "z" else (z + step, seq)
        return pltpu.make_async_remote_copy(
            src_ref=block(part, offset), dst_ref=block(part, offset),
            send_sem=block_send.at[ids[key]], recv_sem=block_recv.at[recv_index(part, there)],
            device_id=target, device_id_type=MESH)

    def guarded(offset, hop, action):
        conds = []
        if offset[2]:
            conds.append(inside(offset[2]))
        if hop[0] == "z":
            conds.append(inside(hop[1]))
        if conds:
            pl.when(functools.reduce(lambda a, b: a & b, conds))(action)
        else:
            action()

    def start(part, offset, hop):
        guarded(offset, hop, lambda: send(part, offset, hop).start())
        pending.append((part, offset, hop))

    opening = [(part, hop) for part in range(3) for hop in forwards(ORDERS[part], (0, 0, 0), depth)]
    opening.sort(key=lambda item: OPENING[item[0]]["xyz".index(item[1][0])])
    for part, hop in opening:
        start(part, (0, 0, 0), hop)
    tok_send.start()
    tok_copy.start()
    turn_send.start()
    turn_copy.start()
    others = []
    for step in range(1, n_seq):
        others.append(pltpu.make_async_remote_copy(
            src_ref=meta_ref, dst_ref=meta_all.at[seq], send_sem=meta_send.at[step],
            recv_sem=meta_recv.at[step], device_id=(z, lax.rem(seq + step, n_seq)),
            device_id_type=MESH))
        others[-1].start()

    def consume(part, offset, initial=False):
        begin, width = part_bounds(half)[part]
        chip = chip_of(offset)
        depth_cols = pl.ds(pl.multiple_of(chip * block_rows, block_rows), block_rows)
        tile = total.shape[0] // 3

        @pl.loop(0, 3)
        def _(index):
            at = pl.ds(pl.multiple_of(index * tile, tile), tile)
            product = jnp.dot(tok_all[at, depth_cols], w_all[chip, :, pl.ds(begin, width)],
                              preferred_element_type=jnp.float32)
            if initial:
                total[at, pl.ds(begin, width)] = product
            else:
                total[at, pl.ds(begin, width)] += product

    def consume_guarded(part, offset):
        if offset[2]:
            pl.when(inside(offset[2]))(lambda: consume(part, offset))
        else:
            consume(part, offset)

    events = []
    for part in range(3):
        for dz in range(1 - depth, depth):
            for dy in range(2):
                for dx in range(2):
                    if (dx, dy, dz) != (0, 0, 0):
                        events.append((part, (dx, dy, dz)))

    def rank(event):
        part, offset = event
        cost = sum(abs(v) * c for v, c in zip(offset, HOP_COSTS[part]))
        return (BASES[part] + cost, part, offset)

    events.sort(key=rank)
    lag = 6
    waiting = []
    ready = False

    def begin_products():
        tok_copy.wait()
        tok_send.wait()
        turn_copy.wait()
        turn_send.wait()
        for part in range(3):
            consume(part, (0, 0, 0), initial=True)

    def turned(at, begin):
        heads = total[at, pl.ds(begin, HEAD_DIM)]
        swapped = pltpu.roll(heads, HEAD_DIM // 2, 1)
        angle = turn_all[at, :]
        return (heads * angle[:, :HEAD_DIM] + swapped * angle[:, HEAD_DIM:]).astype(jnp.bfloat16)

    kv_copy = pltpu.make_async_remote_copy(
        src_ref=kv_out.at[pl.ds(CORES, CORES)], dst_ref=kv_before, send_sem=kv_send,
        recv_sem=kv_recv, device_id=follower, device_id_type=MESH)

    def share_kv():
        for index in range(CORES):
            at = pl.ds(index * rows, rows)
            for begin in range(0, kv_per, HEAD_DIM):
                kv_out[CORES + index, :, pl.ds(begin, HEAD_DIM)] = turned(at, begin)
            kv_out[CORES + index, :, pl.ds(kv_per, kv_per)] = total[
                at, pl.ds(kv_per, kv_per)].astype(jnp.bfloat16)
        pl.when(plane < planes - 1)(lambda: kv_copy.start())

    def use(item):
        consume_guarded(*item)
        left[item[0]] -= 1
        if item[0] == 0 and left[0] == 0:
            share_kv()

    left = [sum(1 for event in events if event[0] == part) for part in range(3)]
    for part, offset in events:
        dz = offset[2]

        def arrive(part=part, offset=offset):
            own = block(part, offset)
            pltpu.make_async_remote_copy(
                src_ref=own, dst_ref=own, send_sem=block_send.at[0],
                recv_sem=block_recv.at[recv_index(part, offset)],
                device_id=partner, device_id_type=MESH).wait_recv()
        if dz:
            pl.when(inside(dz))(arrive)
        else:
            arrive()
        for hop in forwards(ORDERS[part], offset, depth):
            start(part, offset, hop)
        waiting.append((part, offset))
        if len(waiting) > lag and not ready:
            begin_products()
            ready = True
        if ready:
            for item in waiting[:2]:
                use(item)
            del waiting[:2]
    if not ready:
        begin_products()
    for item in waiting:
        use(item)
    for index in range(CORES):
        at = pl.ds(index * rows, rows)
        for begin in range(0, heads_per, HEAD_DIM):
            query_out[index, :, pl.ds(begin, HEAD_DIM)] = turned(at, 2 * kv_per + begin)
    for copy in others:
        copy.wait()
    meta_all[seq] = meta_ref[...]
    meta_out[...] = meta_all[...]

    @pl.when(plane > 0)
    def _():
        kv_copy.wait_recv()
        kv_out[0:CORES] = kv_before[...]

    @pl.when(plane == 0)
    def _():
        kv_out[0:CORES] = jnp.zeros_like(kv_before)

    pl.when(plane < planes - 1)(lambda: kv_copy.wait_send())
    for part, offset, hop in pending:
        guarded(offset, hop, lambda: send(part, offset, hop).wait_send())


def count_sends(depth):
    total = 0
    for order in ORDERS:
        for dz in range(1 - depth, depth):
            for dy in range(2):
                for dx in range(2):
                    total += len(forwards(order, (dx, dy, dz), depth))
    return total


def project(token_rows, qkv_weight, meta, turn):
    depth, n_seq = lax.axis_size("dp"), lax.axis_size("seq")
    rows, model = token_rows.shape
    columns = qkv_weight.shape[1]
    half = columns // CORES
    queries = HEADS // CORES * HEAD_DIM
    kv_width = half - queries
    chips = depth * n_seq // CORES
    block_rows = model // chips
    sends = count_sends(depth)
    recvs = len(ORDERS) * (2 * depth - 1) * 4
    vmem = pl.BlockSpec(memory_space=pltpu.VMEM)
    return pl.pallas_call(
        functools.partial(project_kernel, depth, n_seq),
        out_shape=(jax.ShapeDtypeStruct((CORES, rows, queries), jnp.bfloat16),
                   jax.ShapeDtypeStruct((2 * CORES, rows, kv_width), jnp.bfloat16),
                   jax.ShapeDtypeStruct((n_seq,) + meta.shape, jnp.int32)),
        in_specs=[pl.BlockSpec(memory_space=pl.ANY), pl.BlockSpec(memory_space=pl.ANY),
                  vmem, vmem],
        out_specs=(vmem, vmem, vmem),
        scratch_shapes=[
            pltpu.VMEM((CORES * rows, model), jnp.bfloat16),
            pltpu.VMEM((chips, block_rows, half), jnp.bfloat16),
            pltpu.VMEM((n_seq,) + meta.shape, jnp.int32),
            pltpu.VMEM((CORES * rows, 2 * HEAD_DIM), jnp.float32),
            pltpu.VMEM((CORES * rows, half), jnp.float32),
            pltpu.VMEM((CORES, rows, kv_width), jnp.bfloat16),
            pltpu.SemaphoreType.DMA((5,)),
            pltpu.SemaphoreType.DMA((5,)),
            pltpu.SemaphoreType.DMA((5,)),
            pltpu.SemaphoreType.DMA((n_seq,)),
            pltpu.SemaphoreType.DMA((n_seq,)),
            pltpu.SemaphoreType.DMA((sends,)),
            pltpu.SemaphoreType.DMA((recvs,)),
            pltpu.SemaphoreType.DMA,
            pltpu.SemaphoreType.DMA,
        ],
        compiler_params=pltpu.CompilerParams(
            collective_id=0, has_side_effects=True, vmem_limit_bytes=60 * 2**20),
        cost_estimate=pl.CostEstimate(flops=2 * rows * model * columns,
                                      bytes_accessed=2 * model * columns, transcendentals=0),
    )(token_rows, qkv_weight, meta, turn)


def project_plain(token_rows, qkv_weight, meta, turn):
    n_seq = lax.axis_size("seq")
    rows = token_rows.shape[0]
    core = lax.axis_index("seq") % CORES

    def paired(block):
        other = lax.ppermute(block, "seq", [(i, i ^ 1) for i in range(n_seq)])
        return jnp.where(core == 0, jnp.concatenate([block, other]),
                         jnp.concatenate([other, block]))

    weight = lax.all_gather(qkv_weight, ("dp", "seq"), axis=0, tiled=True)
    heads_per = HEADS // CORES * HEAD_DIM
    kv_per = KV_HEADS // CORES * HEAD_DIM
    pieces = [
        lax.dynamic_slice_in_dim(weight, base + core * width, width, 1)
        for base, width in ((0, heads_per), (HEADS * HEAD_DIM, kv_per),
                            ((HEADS + KV_HEADS) * HEAD_DIM, kv_per))
    ]
    projected = jnp.dot(paired(token_rows), jnp.concatenate(pieces, axis=1),
                        preferred_element_type=jnp.float32)
    angle = paired(turn)

    def turned(flat):
        heads = flat.reshape(flat.shape[0], -1, HEAD_DIM)
        swapped = jnp.roll(heads, HEAD_DIM // 2, axis=2)
        both = heads * angle[:, None, :HEAD_DIM] + swapped * angle[:, None, HEAD_DIM:]
        return both.reshape(flat.shape).astype(jnp.bfloat16)

    queries = turned(projected[:, :heads_per]).reshape(CORES, rows, heads_per)
    keys = turned(projected[:, heads_per : heads_per + kv_per])
    values = projected[:, heads_per + kv_per :].astype(jnp.bfloat16)
    own = jnp.concatenate([keys, values], axis=1)
    before = lax.ppermute(own, "seq", [(i, i + CORES) for i in range(n_seq - CORES)])
    span = jnp.concatenate([before, own]).reshape(2 * CORES, rows, 2 * kv_per)
    return queries, span, lax.all_gather(meta, "seq")


def turns(segment_ids, prefix_len):
    first_row = jnp.sum(
        (segment_ids[None, :] < segment_ids[:, None]).astype(jnp.int32), axis=1)
    index_list = jnp.arange(segment_ids.shape[0], dtype=jnp.int32)
    leading = segment_ids == segment_ids[0]
    position = index_list - first_row + jnp.where(leading, prefix_len, 0)
    half_dim = HEAD_DIM // 2
    frequency = ROPE_BASE ** (-2.0 * jnp.arange(half_dim, dtype=jnp.float32) / HEAD_DIM)
    angles = position.astype(jnp.float32)[:, None] * frequency[None, :]
    cosine, sine = jnp.cos(angles), jnp.sin(angles)
    return jnp.concatenate([cosine, cosine, -sine, sine], axis=1)


def attend_kernel(tile, metas_ref, pair_ref, q_ref, k_ref, v_ref, out_ref):
    block = pl.program_id(0)
    owner = lax.axis_index("seq") // CORES * CORES + block
    count = q_ref.shape[1]
    group = q_ref.shape[2] // HEAD_DIM
    prefix = metas_ref[owner, 2, 0]
    factor = HEAD_DIM ** -0.5 * 1.4426950408889634

    def run(index, remote):
        at = pl.ds(pl.multiple_of(index * tile, tile), tile)
        blocks = remote + 1
        window = pl.ds(block + REACH - remote, blocks)
        keys = k_ref[window].reshape(blocks * count, HEAD_DIM)
        values = v_ref[window].reshape(blocks * count, HEAD_DIM)
        row = pair_ref[owner, pl.ds(0, 1), :]
        columns = lax.broadcasted_iota(jnp.int32, (tile, count), 1)
        lines = lax.broadcasted_iota(jnp.int32, (tile, count), 0) + index * tile
        ids = jnp.sum(jnp.where(columns == lines, row, 0), axis=1, keepdims=True)
        seen = (columns <= lines) & (row == ids)
        if remote:
            back = lax.broadcasted_iota(jnp.int32, (tile, remote * count), 1) - remote * count
            lead = ids == row[:, :1]
            seen = jnp.concatenate([(back >= -prefix) & lead, seen], axis=1)
        parts = [pl.ds(head * HEAD_DIM, HEAD_DIM) for head in range(group)]
        queries = jnp.concatenate([q_ref[0, at, cols] for cols in parts], axis=0)
        scores = lax.dot_general(queries, keys, (((1,), (1,)), ((), ())),
                                 preferred_element_type=jnp.float32)
        scores = scores.reshape(group, tile, blocks * count)
        scores = jnp.where(seen[None], scores, MASKED)
        top = jnp.max(scores, axis=-1, keepdims=True)
        expo = jnp.exp2((scores - top) * factor)
        total = jnp.sum(expo, axis=-1, keepdims=True)
        probs = (expo * (1.0 / total)).astype(jnp.bfloat16)
        out = jnp.dot(probs.reshape(group * tile, blocks * count), values,
                      preferred_element_type=jnp.float32).astype(jnp.bfloat16)
        for head, cols in enumerate(parts):
            out_ref[0, at, cols] = out[head * tile : (head + 1) * tile]

    @pl.loop(0, count // tile)
    def _(index):
        lead = metas_ref[owner, 0, index * tile] == metas_ref[owner, 0, 0]
        remote = jnp.where(lead, prefix, 0)
        for blocks in range(REACH + 1):
            low = remote > (blocks - 1) * count
            high = remote <= blocks * count
            cond = low & high if 0 < blocks < REACH else (high if blocks == 0 else low)
            pl.when(cond)(functools.partial(run, index, blocks))


def attend(queries, span, metas):
    blocks, count, width = queries.shape
    kv_heads = span.shape[2] // HEAD_DIM // 2
    group = width // kv_heads
    tile = 128
    return pl.pallas_call(
        functools.partial(attend_kernel, tile),
        grid=(blocks, kv_heads),
        out_shape=jax.ShapeDtypeStruct(queries.shape, jnp.bfloat16),
        in_specs=[
            pl.BlockSpec(memory_space=pltpu.SMEM), pl.BlockSpec(memory_space=pltpu.VMEM),
            pl.BlockSpec((1, count, group), lambda b, h: (b, 0, h)),
            pl.BlockSpec((span.shape[0], count, HEAD_DIM), lambda b, h: (0, 0, h)),
            pl.BlockSpec((span.shape[0], count, HEAD_DIM), lambda b, h: (0, 0, kv_heads + h)),
        ],
        out_specs=pl.BlockSpec((1, count, group), lambda b, h: (b, 0, h)),
        compiler_params=pltpu.CompilerParams(vmem_limit_bytes=60 * 2**20),
        cost_estimate=pl.CostEstimate(
            flops=4 * blocks * count * width * count * (REACH + 1),
            bytes_accessed=8 * blocks * count * width, transcendentals=0),
    )(metas, metas, queries, span, span)


def on_device(tokens, qkv_weight, segments, destination, doc_prefix):
    n_seq = lax.axis_size("seq")
    me = lax.axis_index("seq")
    count = tokens.shape[1]
    capacity = count // min(n_seq, 16)
    target = destination[0]
    owner = lax.div(target, count)
    index_list = jnp.arange(count, dtype=jnp.int32)
    earlier = (owner[None, :] == owner[:, None]) & (index_list[None, :] < index_list[:, None])
    core = lax.rem(me, CORES)
    slot = (owner * CORES + core) * capacity + jnp.sum(earlier.astype(jnp.int32), axis=1)
    prefix_row = jnp.broadcast_to(doc_prefix[0], (count,))
    meta = jnp.stack([segments[0], target, prefix_row, slot] + [slot] * (META_ROWS - 4))
    turn = turns(segments[0], doc_prefix[0, 0])
    planar = n_seq == 4 * CORES
    queries, span, metas = (project if planar else project_plain)(
        tokens[0], qkv_weight, meta, turn)
    heads_per = queries.shape[2]
    heads_out = attend(queries, span, metas)

    slots = jnp.arange(n_seq * CORES * capacity, dtype=jnp.int32)
    pair_slots = lax.dynamic_slice_in_dim(metas[:, 3], me - core, CORES, 0).reshape(1, -1)
    chosen = (slots[:, None] == pair_slots).astype(jnp.bfloat16)
    send_rows = jnp.dot(chosen, heads_out.reshape(CORES * count, heads_per),
                        preferred_element_type=jnp.float32).astype(jnp.bfloat16)
    got = lax.all_to_all(send_rows.reshape(n_seq, CORES * capacity, heads_per), "seq",
                         split_axis=0, concat_axis=0, tiled=True)
    got = got.reshape(n_seq // CORES, CORES, CORES, capacity, heads_per)

    wanted = slots.reshape(n_seq, CORES, capacity)[0] + me * CORES * capacity
    wanted = jnp.tile(wanted, (n_seq // CORES, 1))
    match = metas[:, 3][:, None, :] == wanted[:, :, None]
    places = jnp.sum(
        jnp.where(match, lax.rem(metas[:, 1], count)[:, None, :] + 1, 0), axis=2) - 1
    places = places.reshape(-1)
    put = (index_list[:, None] == places[None, :]).astype(jnp.bfloat16)
    halves = [
        jnp.dot(put, got[:, c].reshape(n_seq * capacity, heads_per),
                preferred_element_type=jnp.float32).astype(jnp.bfloat16)
        for c in range(CORES)
    ]
    return jnp.concatenate(halves, axis=1)[None]


def solution(mesh):
    placed = (
        P("dp", "seq", None),
        P(("dp", "seq"), None),
        P("dp", "seq"),
        P("dp", "seq"),
        P("dp", "seq"),
    )
    return jax.shard_map(
        on_device, mesh=mesh, in_specs=placed, out_specs=P("dp", "seq", None), check_vma=False
    )
```

```python
import functools

import jax
import jax.numpy as jnp
from jax import lax
from jax.experimental import pallas as pl
from jax.experimental.pallas import tpu as pltpu
from jax.sharding import PartitionSpec as P

HEADS = 16
KV_HEADS = 4
HEAD_DIM = 128
REACH = 2
ROPE_BASE = 500000.0
MASKED = -1e30
CORES = 2
MESH = pl.DeviceIdType.MESH
META_ROWS = 8

ORDERS = ("zxy", "zyx", "xyz")
BASES = (-1.5, -2.0, -2.5)
HOP_COSTS = ((4.25, 3.75, 0.75), (4.75, 4.25, 0.75), (3.75, 2.25, 3.0))
OPENING = ((8.0, -5.5, 6.0), (4.0, 2.0, -11.0), (-1.5, 0.0, 11.5))


def part_bounds(width):
    unit = width // 12
    return ((0, 4 * unit), (4 * unit, 5 * unit), (9 * unit, 3 * unit))


def forwards(order, offset, depth):
    delta = dict(zip("xyz", offset))
    last = max([order.index(a) for a in order if delta[a]], default=-1)
    hops = []
    for index, axis in enumerate(order):
        if index < last:
            continue
        if axis == "z":
            steps = (1, -1) if delta["z"] == 0 else ((1,) if delta["z"] < 0 else (-1,))
            for step in steps:
                if abs(delta["z"] - step) < depth:
                    hops.append(("z", step, (delta["x"], delta["y"], delta["z"] - step)))
        elif index > last:
            there = dict(delta)
            there[axis] = 1
            hops.append((axis, 1, (there["x"], there["y"], there["z"])))
    return hops


def project_kernel(depth, n_seq, tok_ref, w_ref, meta_ref, turn_ref, query_out, kv_out, meta_out,
                   tok_all, w_all, meta_all, turn_all, total, kv_before, local_sem, pair_send,
                   pair_recv, meta_send, meta_recv, block_send, block_recv, kv_send, kv_recv):
    z = lax.axis_index("dp")
    seq = lax.axis_index("seq")
    core = lax.rem(seq, CORES)
    plane = seq // CORES
    x = lax.rem(plane, 2)
    y = plane // 2
    rows, model = tok_ref.shape
    shard = w_ref.shape[0]
    half = total.shape[1]
    planes = n_seq // CORES
    heads_per = HEADS // CORES * HEAD_DIM
    kv_per = KV_HEADS // CORES * HEAD_DIM
    block_rows = shard * CORES
    partner = (z, seq + 1 - 2 * core)
    side = {
        "x": (z, (y * 2 + 1 - x) * CORES + core),
        "y": (z, ((1 - y) * 2 + x) * CORES + core),
    }
    follower = (z, lax.rem(seq + CORES, n_seq))

    def inside(dz):
        return (z + dz >= 0) & (z + dz < depth)

    barrier = pltpu.get_barrier_semaphore()
    for step in range(1, n_seq):
        pl.semaphore_signal(barrier, inc=1, device_id=(z, lax.rem(seq + step, n_seq)),
                            device_id_type=MESH)
    for step in (1, -1):
        @pl.when(inside(step))
        def _(step=step):
            pl.semaphore_signal(barrier, inc=1, device_id=(z + step, seq), device_id_type=MESH)
    peers = n_seq - 1 + jnp.where(z > 0, 1, 0) + jnp.where(z < depth - 1, 1, 0)
    pl.semaphore_wait(barrier, peers)

    def chip_of(offset):
        dx, dy, dz = offset
        cx = 1 - x if dx else x
        cy = 1 - y if dy else y
        return ((z + dz) * 2 + cy) * 2 + cx

    mine = chip_of((0, 0, 0))
    own_rows = pl.ds(pl.multiple_of(core * shard, shard), shard)
    slices = ((HEADS * HEAD_DIM, 0, kv_per),
              ((HEADS + KV_HEADS) * HEAD_DIM, kv_per, kv_per),
              (0, 2 * kv_per, heads_per))
    first = []
    for index, (base, place, width) in enumerate(slices):
        there = pl.ds(pl.multiple_of(base + (1 - core) * width, 128), width)
        here = pl.ds(pl.multiple_of(base + core * width, 128), width)
        first.append(pltpu.make_async_remote_copy(
            src_ref=w_ref.at[:, there], dst_ref=w_all.at[mine, own_rows, pl.ds(place, width)],
            send_sem=pair_send.at[index], recv_sem=pair_recv.at[index],
            device_id=partner, device_id_type=MESH))
        first.append(pltpu.make_async_copy(
            w_ref.at[:, here], w_all.at[mine, own_rows, pl.ds(place, width)],
            local_sem.at[index]))
    for copy in first:
        copy.start()
    tok_rows = pl.ds(pl.multiple_of(core * rows, rows), rows)
    tok_send = pltpu.make_async_remote_copy(
        src_ref=tok_ref, dst_ref=tok_all.at[tok_rows, :], send_sem=pair_send.at[3],
        recv_sem=pair_recv.at[3], device_id=partner, device_id_type=MESH)
    tok_copy = pltpu.make_async_copy(tok_ref, tok_all.at[tok_rows, :], local_sem.at[3])
    turn_send = pltpu.make_async_remote_copy(
        src_ref=turn_ref, dst_ref=turn_all.at[tok_rows, :], send_sem=pair_send.at[4],
        recv_sem=pair_recv.at[4], device_id=partner, device_id_type=MESH)
    turn_copy = pltpu.make_async_copy(turn_ref, turn_all.at[tok_rows, :], local_sem.at[4])
    for copy in first:
        copy.wait()

    ids = {}
    pending = []

    def block(part, offset):
        start, width = part_bounds(half)[part]
        return w_all.at[chip_of(offset), :, pl.ds(start, width)]

    def recv_index(part, offset):
        dx, dy, dz = offset
        return ((part * (2 * depth - 1) + dz + depth - 1) * 2 + dy) * 2 + dx

    def send(part, offset, hop):
        axis, step, there = hop
        key = (part, offset, axis, step)
        ids.setdefault(key, len(ids))
        target = side[axis] if axis != "z" else (z + step, seq)
        return pltpu.make_async_remote_copy(
            src_ref=block(part, offset), dst_ref=block(part, offset),
            send_sem=block_send.at[ids[key]], recv_sem=block_recv.at[recv_index(part, there)],
            device_id=target, device_id_type=MESH)

    def guarded(offset, hop, action):
        conds = []
        if offset[2]:
            conds.append(inside(offset[2]))
        if hop[0] == "z":
            conds.append(inside(hop[1]))
        if conds:
            pl.when(functools.reduce(lambda a, b: a & b, conds))(action)
        else:
            action()

    def start(part, offset, hop):
        guarded(offset, hop, lambda: send(part, offset, hop).start())
        pending.append((part, offset, hop))

    opening = [(part, hop) for part in range(3) for hop in forwards(ORDERS[part], (0, 0, 0), depth)]
    opening.sort(key=lambda item: OPENING[item[0]]["xyz".index(item[1][0])])
    for part, hop in opening:
        start(part, (0, 0, 0), hop)
    tok_send.start()
    tok_copy.start()
    turn_send.start()
    turn_copy.start()
    others = []
    for step in range(1, n_seq):
        others.append(pltpu.make_async_remote_copy(
            src_ref=meta_ref, dst_ref=meta_all.at[seq], send_sem=meta_send.at[step],
            recv_sem=meta_recv.at[step], device_id=(z, lax.rem(seq + step, n_seq)),
            device_id_type=MESH))
        others[-1].start()

    def consume(part, offset, initial=False):
        begin, width = part_bounds(half)[part]
        chip = chip_of(offset)
        depth_cols = pl.ds(pl.multiple_of(chip * block_rows, block_rows), block_rows)
        tile = total.shape[0] // 3

        @pl.loop(0, 3)
        def _(index):
            at = pl.ds(pl.multiple_of(index * tile, tile), tile)
            product = jnp.dot(tok_all[at, depth_cols], w_all[chip, :, pl.ds(begin, width)],
                              preferred_element_type=jnp.float32)
            if initial:
                total[at, pl.ds(begin, width)] = product
            else:
                total[at, pl.ds(begin, width)] += product

    def consume_guarded(part, offset):
        if offset[2]:
            pl.when(inside(offset[2]))(lambda: consume(part, offset))
        else:
            consume(part, offset)

    events = []
    for part in range(3):
        for dz in range(1 - depth, depth):
            for dy in range(2):
                for dx in range(2):
                    if (dx, dy, dz) != (0, 0, 0):
                        events.append((part, (dx, dy, dz)))

    def rank(event):
        part, offset = event
        cost = sum(abs(v) * c for v, c in zip(offset, HOP_COSTS[part]))
        return (BASES[part] + cost, part, offset)

    events.sort(key=rank)
    lag = 6
    waiting = []
    ready = False

    def begin_products():
        tok_copy.wait()
        tok_send.wait()
        turn_copy.wait()
        turn_send.wait()
        for part in range(3):
            consume(part, (0, 0, 0), initial=True)

    def turned(at, begin):
        heads = total[at, pl.ds(begin, HEAD_DIM)]
        swapped = pltpu.roll(heads, HEAD_DIM // 2, 1)
        angle = turn_all[at, :]
        return (heads * angle[:, :HEAD_DIM] + swapped * angle[:, HEAD_DIM:]).astype(jnp.bfloat16)

    kv_copy = pltpu.make_async_remote_copy(
        src_ref=kv_out.at[pl.ds(CORES, CORES)], dst_ref=kv_before, send_sem=kv_send,
        recv_sem=kv_recv, device_id=follower, device_id_type=MESH)

    def share_kv():
        for index in range(CORES):
            at = pl.ds(index * rows, rows)
            for begin in range(0, kv_per, HEAD_DIM):
                kv_out[CORES + index, :, pl.ds(begin, HEAD_DIM)] = turned(at, begin)
            kv_out[CORES + index, :, pl.ds(kv_per, kv_per)] = total[
                at, pl.ds(kv_per, kv_per)].astype(jnp.bfloat16)
        pl.when(plane < planes - 1)(lambda: kv_copy.start())

    def use(item):
        consume_guarded(*item)
        left[item[0]] -= 1
        if item[0] == 0 and left[0] == 0:
            share_kv()

    left = [sum(1 for event in events if event[0] == part) for part in range(3)]
    for part, offset in events:
        dz = offset[2]

        def arrive(part=part, offset=offset):
            own = block(part, offset)
            pltpu.make_async_remote_copy(
                src_ref=own, dst_ref=own, send_sem=block_send.at[0],
                recv_sem=block_recv.at[recv_index(part, offset)],
                device_id=partner, device_id_type=MESH).wait_recv()
        if dz:
            pl.when(inside(dz))(arrive)
        else:
            arrive()
        for hop in forwards(ORDERS[part], offset, depth):
            start(part, offset, hop)
        waiting.append((part, offset))
        if len(waiting) > lag and not ready:
            begin_products()
            ready = True
        if ready:
            for item in waiting[:2]:
                use(item)
            del waiting[:2]
    if not ready:
        begin_products()
    for item in waiting:
        use(item)
    for index in range(CORES):
        at = pl.ds(index * rows, rows)
        for begin in range(0, heads_per, HEAD_DIM):
            query_out[index, :, pl.ds(begin, HEAD_DIM)] = turned(at, 2 * kv_per + begin)
    for copy in others:
        copy.wait()
    meta_all[seq] = meta_ref[...]
    meta_out[...] = meta_all[...]

    @pl.when(plane > 0)
    def _():
        kv_copy.wait_recv()
        kv_out[0:CORES] = kv_before[...]

    @pl.when(plane == 0)
    def _():
        kv_out[0:CORES] = jnp.zeros_like(kv_before)

    pl.when(plane < planes - 1)(lambda: kv_copy.wait_send())
    for part, offset, hop in pending:
        guarded(offset, hop, lambda: send(part, offset, hop).wait_send())


def count_sends(depth):
    total = 0
    for order in ORDERS:
        for dz in range(1 - depth, depth):
            for dy in range(2):
                for dx in range(2):
                    total += len(forwards(order, (dx, dy, dz), depth))
    return total


def project(token_rows, qkv_weight, meta, turn):
    depth, n_seq = lax.axis_size("dp"), lax.axis_size("seq")
    rows, model = token_rows.shape
    columns = qkv_weight.shape[1]
    half = columns // CORES
    queries = HEADS // CORES * HEAD_DIM
    kv_width = half - queries
    chips = depth * n_seq // CORES
    block_rows = model // chips
    sends = count_sends(depth)
    recvs = len(ORDERS) * (2 * depth - 1) * 4
    vmem = pl.BlockSpec(memory_space=pltpu.VMEM)
    return pl.pallas_call(
        functools.partial(project_kernel, depth, n_seq),
        out_shape=(jax.ShapeDtypeStruct((CORES, rows, queries), jnp.bfloat16),
                   jax.ShapeDtypeStruct((2 * CORES, rows, kv_width), jnp.bfloat16),
                   jax.ShapeDtypeStruct((n_seq,) + meta.shape, jnp.int32)),
        in_specs=[pl.BlockSpec(memory_space=pl.ANY), pl.BlockSpec(memory_space=pl.ANY),
                  vmem, vmem],
        out_specs=(vmem, vmem, vmem),
        scratch_shapes=[
            pltpu.VMEM((CORES * rows, model), jnp.bfloat16),
            pltpu.VMEM((chips, block_rows, half), jnp.bfloat16),
            pltpu.VMEM((n_seq,) + meta.shape, jnp.int32),
            pltpu.VMEM((CORES * rows, 2 * HEAD_DIM), jnp.float32),
            pltpu.VMEM((CORES * rows, half), jnp.float32),
            pltpu.VMEM((CORES, rows, kv_width), jnp.bfloat16),
            pltpu.SemaphoreType.DMA((5,)),
            pltpu.SemaphoreType.DMA((5,)),
            pltpu.SemaphoreType.DMA((5,)),
            pltpu.SemaphoreType.DMA((n_seq,)),
            pltpu.SemaphoreType.DMA((n_seq,)),
            pltpu.SemaphoreType.DMA((sends,)),
            pltpu.SemaphoreType.DMA((recvs,)),
            pltpu.SemaphoreType.DMA,
            pltpu.SemaphoreType.DMA,
        ],
        compiler_params=pltpu.CompilerParams(
            collective_id=0, has_side_effects=True, vmem_limit_bytes=60 * 2**20),
        cost_estimate=pl.CostEstimate(flops=2 * rows * model * columns,
                                      bytes_accessed=2 * model * columns, transcendentals=0),
    )(token_rows, qkv_weight, meta, turn)


def project_plain(token_rows, qkv_weight, meta, turn):
    n_seq = lax.axis_size("seq")
    rows = token_rows.shape[0]
    core = lax.axis_index("seq") % CORES

    def paired(block):
        other = lax.ppermute(block, "seq", [(i, i ^ 1) for i in range(n_seq)])
        return jnp.where(core == 0, jnp.concatenate([block, other]),
                         jnp.concatenate([other, block]))

    weight = lax.all_gather(qkv_weight, ("dp", "seq"), axis=0, tiled=True)
    heads_per = HEADS // CORES * HEAD_DIM
    kv_per = KV_HEADS // CORES * HEAD_DIM
    pieces = [
        lax.dynamic_slice_in_dim(weight, base + core * width, width, 1)
        for base, width in ((0, heads_per), (HEADS * HEAD_DIM, kv_per),
                            ((HEADS + KV_HEADS) * HEAD_DIM, kv_per))
    ]
    projected = jnp.dot(paired(token_rows), jnp.concatenate(pieces, axis=1),
                        preferred_element_type=jnp.float32)
    angle = paired(turn)

    def turned(flat):
        heads = flat.reshape(flat.shape[0], -1, HEAD_DIM)
        swapped = jnp.roll(heads, HEAD_DIM // 2, axis=2)
        both = heads * angle[:, None, :HEAD_DIM] + swapped * angle[:, None, HEAD_DIM:]
        return both.reshape(flat.shape).astype(jnp.bfloat16)

    queries = turned(projected[:, :heads_per]).reshape(CORES, rows, heads_per)
    keys = turned(projected[:, heads_per : heads_per + kv_per])
    values = projected[:, heads_per + kv_per :].astype(jnp.bfloat16)
    own = jnp.concatenate([keys, values], axis=1)
    before = lax.ppermute(own, "seq", [(i, i + CORES) for i in range(n_seq - CORES)])
    span = jnp.concatenate([before, own]).reshape(2 * CORES, rows, 2 * kv_per)
    return queries, span, lax.all_gather(meta, "seq")


def turns(segment_ids, prefix_len):
    first_row = jnp.sum(
        (segment_ids[None, :] < segment_ids[:, None]).astype(jnp.int32), axis=1)
    index_list = jnp.arange(segment_ids.shape[0], dtype=jnp.int32)
    leading = segment_ids == segment_ids[0]
    position = index_list - first_row + jnp.where(leading, prefix_len, 0)
    half_dim = HEAD_DIM // 2
    frequency = ROPE_BASE ** (-2.0 * jnp.arange(half_dim, dtype=jnp.float32) / HEAD_DIM)
    angles = position.astype(jnp.float32)[:, None] * frequency[None, :]
    cosine, sine = jnp.cos(angles), jnp.sin(angles)
    return jnp.concatenate([cosine, cosine, -sine, sine], axis=1)


def attend_kernel(tile, metas_ref, pair_ref, q_ref, k_ref, v_ref, out_ref, rows_ref):
    block = pl.program_id(0)
    owner = lax.axis_index("seq") // CORES * CORES + block
    count = q_ref.shape[1]
    group = q_ref.shape[2] // HEAD_DIM
    prefix = metas_ref[owner, 2, 0]
    factor = HEAD_DIM ** -0.5 * 1.4426950408889634

    def run(index, remote):
        at = pl.ds(pl.multiple_of(index * tile, tile), tile)
        blocks = remote + 1
        window = pl.ds(block + REACH - remote, blocks)
        keys = k_ref[window].reshape(blocks * count, HEAD_DIM)
        values = v_ref[window].reshape(blocks * count, HEAD_DIM)
        row = pair_ref[owner, pl.ds(0, 1), :]
        columns = lax.broadcasted_iota(jnp.int32, (tile, count), 1)
        lines = lax.broadcasted_iota(jnp.int32, (tile, count), 0) + index * tile
        ids = jnp.sum(jnp.where(columns == lines, row, 0), axis=1, keepdims=True)
        seen = (columns <= lines) & (row == ids)
        if remote:
            back = lax.broadcasted_iota(jnp.int32, (tile, remote * count), 1) - remote * count
            lead = ids == row[:, :1]
            seen = jnp.concatenate([(back >= -prefix) & lead, seen], axis=1)
        parts = [pl.ds(head * HEAD_DIM, HEAD_DIM) for head in range(group)]
        queries = jnp.concatenate([q_ref[0, at, cols] for cols in parts], axis=0)
        scores = lax.dot_general(queries, keys, (((1,), (1,)), ((), ())),
                                 preferred_element_type=jnp.float32)
        scores = scores.reshape(group, tile, blocks * count)
        scores = jnp.where(seen[None], scores, MASKED)
        top = jnp.max(scores, axis=-1, keepdims=True)
        expo = jnp.exp2((scores - top) * factor)
        total = jnp.sum(expo, axis=-1, keepdims=True)
        out = jnp.dot(expo.astype(jnp.bfloat16).reshape(group * tile, blocks * count), values,
                      preferred_element_type=jnp.float32)
        out = (out.reshape(group, tile, HEAD_DIM) * (1.0 / total)).astype(jnp.bfloat16)
        for head, cols in enumerate(parts):
            rows_ref[at, cols] = out[head]

    @pl.loop(0, count // tile)
    def _(index):
        lead = metas_ref[owner, 0, index * tile] == metas_ref[owner, 0, 0]
        remote = jnp.where(lead, prefix, 0)
        for blocks in range(REACH + 1):
            low = remote > (blocks - 1) * count
            high = remote <= blocks * count
            cond = low & high if 0 < blocks < REACH else (high if blocks == 0 else low)
            pl.when(cond)(functools.partial(run, index, blocks))


    devices, _, capacity, width = out_ref.shape
    key = lax.broadcasted_iota(jnp.int32, (devices * capacity, count), 0)
    key = key // capacity * (CORES * capacity) + block * capacity + key % capacity
    chosen = jnp.where(key == pair_ref[owner, pl.ds(3, 1), :], 1.0, 0.0).astype(jnp.bfloat16)
    sent = jnp.dot(chosen, rows_ref[...], preferred_element_type=jnp.float32)
    out_ref[...] = sent.reshape(devices, 1, capacity, width).astype(jnp.bfloat16)


def attend(head, capacity, queries, span, metas):
    blocks, count, width = queries.shape
    n_seq = metas.shape[0]
    kv_heads = span.shape[2] // HEAD_DIM // 2
    group = width // kv_heads
    return pl.pallas_call(
        functools.partial(attend_kernel, 128),
        grid=(blocks,),
        out_shape=jax.ShapeDtypeStruct((n_seq, blocks, capacity, group), jnp.bfloat16),
        in_specs=[
            pl.BlockSpec(memory_space=pltpu.SMEM), pl.BlockSpec(memory_space=pltpu.VMEM),
            pl.BlockSpec((1, count, group), lambda b: (b, 0, head)),
            pl.BlockSpec((span.shape[0], count, HEAD_DIM), lambda b: (0, 0, head)),
            pl.BlockSpec((span.shape[0], count, HEAD_DIM), lambda b: (0, 0, kv_heads + head)),
        ],
        out_specs=pl.BlockSpec((n_seq, 1, capacity, group), lambda b: (0, b, 0, 0)),
        scratch_shapes=[pltpu.VMEM((count, group), jnp.bfloat16)],
        compiler_params=pltpu.CompilerParams(vmem_limit_bytes=60 * 2**20),
        cost_estimate=pl.CostEstimate(
            flops=4 * blocks * count * group * count * (REACH + 1),
            bytes_accessed=8 * blocks * count * group, transcendentals=0),
    )(metas, metas, queries, span, span)


def on_device(tokens, qkv_weight, segments, destination, doc_prefix):
    n_seq = lax.axis_size("seq")
    me = lax.axis_index("seq")
    count = tokens.shape[1]
    capacity = count // min(n_seq, 16)
    target = destination[0]
    owner = lax.div(target, count)
    index_list = jnp.arange(count, dtype=jnp.int32)
    earlier = (owner[None, :] == owner[:, None]) & (index_list[None, :] < index_list[:, None])
    core = lax.rem(me, CORES)
    slot = (owner * CORES + core) * capacity + jnp.sum(earlier.astype(jnp.int32), axis=1)
    prefix_row = jnp.broadcast_to(doc_prefix[0], (count,))
    meta = jnp.stack([segments[0], target, prefix_row, slot] + [slot] * (META_ROWS - 4))
    turn = turns(segments[0], doc_prefix[0, 0])
    planar = n_seq == 4 * CORES
    queries, span, metas = (project if planar else project_plain)(
        tokens[0], qkv_weight, meta, turn)
    kv_heads = KV_HEADS // CORES
    group = queries.shape[2] // kv_heads
    got = []
    for head in range(kv_heads):
        sent = attend(head, capacity, queries, span, metas)
        here = lax.all_to_all(sent.reshape(n_seq, CORES * capacity, group), "seq",
                              split_axis=0, concat_axis=0, tiled=True)
        got.append(here.reshape(n_seq // CORES, CORES, CORES, capacity, group))

    wanted = jnp.arange(CORES * capacity, dtype=jnp.int32).reshape(CORES, capacity)
    wanted = wanted + me * CORES * capacity
    wanted = jnp.tile(wanted, (n_seq // CORES, 1))
    match = metas[:, 3][:, None, :] == wanted[:, :, None]
    places = jnp.sum(
        jnp.where(match, lax.rem(metas[:, 1], count)[:, None, :] + 1, 0), axis=2) - 1
    places = places.reshape(-1)
    put = (index_list[:, None] == places[None, :]).astype(jnp.bfloat16)
    halves = [
        jnp.dot(put, got[head][:, c].reshape(n_seq * capacity, group),
                preferred_element_type=jnp.float32).astype(jnp.bfloat16)
        for c in range(CORES)
        for head in range(kv_heads)
    ]
    return jnp.concatenate(halves, axis=1)[None]


def solution(mesh):
    placed = (
        P("dp", "seq", None),
        P(("dp", "seq"), None),
        P("dp", "seq"),
        P("dp", "seq"),
        P("dp", "seq"),
    )
    return jax.shard_map(
        on_device, mesh=mesh, in_specs=placed, out_specs=P("dp", "seq", None), check_vma=False
    )
```

```python
import functools

import jax
import jax.numpy as jnp
from jax import lax
from jax.experimental import pallas as pl
from jax.experimental.pallas import tpu as pltpu
from jax.sharding import PartitionSpec as P

HEADS = 16
KV_HEADS = 4
HEAD_DIM = 128
REACH = 2
ROPE_BASE = 500000.0
MASKED = -1e30
CORES = 2
MESH = pl.DeviceIdType.MESH
META_ROWS = 8

ORDERS = ("zxy", "zyx", "xyz")
BASES = (-1.5, -2.0, -2.5)
HOP_COSTS = ((4.25, 3.75, 0.75), (4.75, 4.25, 0.75), (3.75, 2.25, 3.0))
OPENING = ((8.0, -5.5, 6.0), (4.0, 2.0, -11.0), (-1.5, 0.0, 11.5))


def part_bounds(width):
    unit = width // 12
    return ((0, 4 * unit), (4 * unit, 5 * unit), (9 * unit, 3 * unit))


def forwards(order, offset, depth):
    delta = dict(zip("xyz", offset))
    last = max([order.index(a) for a in order if delta[a]], default=-1)
    hops = []
    for index, axis in enumerate(order):
        if index < last:
            continue
        if axis == "z":
            steps = (1, -1) if delta["z"] == 0 else ((1,) if delta["z"] < 0 else (-1,))
            for step in steps:
                if abs(delta["z"] - step) < depth:
                    hops.append(("z", step, (delta["x"], delta["y"], delta["z"] - step)))
        elif index > last:
            there = dict(delta)
            there[axis] = 1
            hops.append((axis, 1, (there["x"], there["y"], there["z"])))
    return hops


def project_kernel(depth, n_seq, tok_ref, w_ref, meta_ref, turn_ref, query_out, kv_out, meta_out,
                   tok_all, w_all, meta_all, turn_all, total, kv_before, local_sem, pair_send,
                   pair_recv, meta_send, meta_recv, block_send, block_recv, kv_send, kv_recv):
    z = lax.axis_index("dp")
    seq = lax.axis_index("seq")
    core = lax.rem(seq, CORES)
    plane = seq // CORES
    x = lax.rem(plane, 2)
    y = plane // 2
    rows, model = tok_ref.shape
    shard = w_ref.shape[0]
    half = total.shape[1]
    planes = n_seq // CORES
    heads_per = HEADS // CORES * HEAD_DIM
    kv_per = KV_HEADS // CORES * HEAD_DIM
    block_rows = shard * CORES
    partner = (z, seq + 1 - 2 * core)
    side = {
        "x": (z, (y * 2 + 1 - x) * CORES + core),
        "y": (z, ((1 - y) * 2 + x) * CORES + core),
    }
    follower = (z, lax.rem(seq + CORES, n_seq))

    def inside(dz):
        return (z + dz >= 0) & (z + dz < depth)

    barrier = pltpu.get_barrier_semaphore()
    for step in range(1, n_seq):
        pl.semaphore_signal(barrier, inc=1, device_id=(z, lax.rem(seq + step, n_seq)),
                            device_id_type=MESH)
    for step in (1, -1):
        @pl.when(inside(step))
        def _(step=step):
            pl.semaphore_signal(barrier, inc=1, device_id=(z + step, seq), device_id_type=MESH)
    peers = n_seq - 1 + jnp.where(z > 0, 1, 0) + jnp.where(z < depth - 1, 1, 0)
    pl.semaphore_wait(barrier, peers)

    def chip_of(offset):
        dx, dy, dz = offset
        cx = 1 - x if dx else x
        cy = 1 - y if dy else y
        return ((z + dz) * 2 + cy) * 2 + cx

    mine = chip_of((0, 0, 0))
    own_rows = pl.ds(pl.multiple_of(core * shard, shard), shard)
    slices = ((HEADS * HEAD_DIM, 0, kv_per),
              ((HEADS + KV_HEADS) * HEAD_DIM, kv_per, kv_per),
              (0, 2 * kv_per, heads_per))
    first = []
    for index, (base, place, width) in enumerate(slices):
        there = pl.ds(pl.multiple_of(base + (1 - core) * width, 128), width)
        here = pl.ds(pl.multiple_of(base + core * width, 128), width)
        first.append(pltpu.make_async_remote_copy(
            src_ref=w_ref.at[:, there], dst_ref=w_all.at[mine, own_rows, pl.ds(place, width)],
            send_sem=pair_send.at[index], recv_sem=pair_recv.at[index],
            device_id=partner, device_id_type=MESH))
        first.append(pltpu.make_async_copy(
            w_ref.at[:, here], w_all.at[mine, own_rows, pl.ds(place, width)],
            local_sem.at[index]))
    for copy in first:
        copy.start()
    tok_rows = pl.ds(pl.multiple_of(core * rows, rows), rows)
    tok_send = pltpu.make_async_remote_copy(
        src_ref=tok_ref, dst_ref=tok_all.at[tok_rows, :], send_sem=pair_send.at[3],
        recv_sem=pair_recv.at[3], device_id=partner, device_id_type=MESH)
    tok_copy = pltpu.make_async_copy(tok_ref, tok_all.at[tok_rows, :], local_sem.at[3])
    turn_send = pltpu.make_async_remote_copy(
        src_ref=turn_ref, dst_ref=turn_all.at[tok_rows, :], send_sem=pair_send.at[4],
        recv_sem=pair_recv.at[4], device_id=partner, device_id_type=MESH)
    turn_copy = pltpu.make_async_copy(turn_ref, turn_all.at[tok_rows, :], local_sem.at[4])
    for copy in first:
        copy.wait()

    ids = {}
    pending = []

    def block(part, offset):
        start, width = part_bounds(half)[part]
        return w_all.at[chip_of(offset), :, pl.ds(start, width)]

    def recv_index(part, offset):
        dx, dy, dz = offset
        return ((part * (2 * depth - 1) + dz + depth - 1) * 2 + dy) * 2 + dx

    def send(part, offset, hop):
        axis, step, there = hop
        key = (part, offset, axis, step)
        ids.setdefault(key, len(ids))
        target = side[axis] if axis != "z" else (z + step, seq)
        return pltpu.make_async_remote_copy(
            src_ref=block(part, offset), dst_ref=block(part, offset),
            send_sem=block_send.at[ids[key]], recv_sem=block_recv.at[recv_index(part, there)],
            device_id=target, device_id_type=MESH)

    def guarded(offset, hop, action):
        conds = []
        if offset[2]:
            conds.append(inside(offset[2]))
        if hop[0] == "z":
            conds.append(inside(hop[1]))
        if conds:
            pl.when(functools.reduce(lambda a, b: a & b, conds))(action)
        else:
            action()

    def start(part, offset, hop):
        guarded(offset, hop, lambda: send(part, offset, hop).start())
        pending.append((part, offset, hop))

    opening = [(part, hop) for part in range(3) for hop in forwards(ORDERS[part], (0, 0, 0), depth)]
    opening.sort(key=lambda item: OPENING[item[0]]["xyz".index(item[1][0])])
    for part, hop in opening:
        start(part, (0, 0, 0), hop)
    tok_send.start()
    tok_copy.start()
    turn_send.start()
    turn_copy.start()
    others = []
    for step in range(1, n_seq):
        others.append(pltpu.make_async_remote_copy(
            src_ref=meta_ref, dst_ref=meta_all.at[seq], send_sem=meta_send.at[step],
            recv_sem=meta_recv.at[step], device_id=(z, lax.rem(seq + step, n_seq)),
            device_id_type=MESH))
        others[-1].start()

    def consume(part, offset, initial=False):
        begin, width = part_bounds(half)[part]
        chip = chip_of(offset)
        depth_cols = pl.ds(pl.multiple_of(chip * block_rows, block_rows), block_rows)
        tile = total.shape[0] // 3

        @pl.loop(0, 3)
        def _(index):
            at = pl.ds(pl.multiple_of(index * tile, tile), tile)
            product = jnp.dot(tok_all[at, depth_cols], w_all[chip, :, pl.ds(begin, width)],
                              preferred_element_type=jnp.float32)
            if initial:
                total[at, pl.ds(begin, width)] = product
            else:
                total[at, pl.ds(begin, width)] += product

    def consume_guarded(part, offset):
        if offset[2]:
            pl.when(inside(offset[2]))(lambda: consume(part, offset))
        else:
            consume(part, offset)

    events = []
    for part in range(3):
        for dz in range(1 - depth, depth):
            for dy in range(2):
                for dx in range(2):
                    if (dx, dy, dz) != (0, 0, 0):
                        events.append((part, (dx, dy, dz)))

    def rank(event):
        part, offset = event
        cost = sum(abs(v) * c for v, c in zip(offset, HOP_COSTS[part]))
        return (BASES[part] + cost, part, offset)

    events.sort(key=rank)
    lag = 6
    waiting = []
    ready = False

    def begin_products():
        tok_copy.wait()
        tok_send.wait()
        turn_copy.wait()
        turn_send.wait()
        for part in range(3):
            consume(part, (0, 0, 0), initial=True)

    def turned(at, begin):
        heads = total[at, pl.ds(begin, HEAD_DIM)]
        swapped = pltpu.roll(heads, HEAD_DIM // 2, 1)
        angle = turn_all[at, :]
        return (heads * angle[:, :HEAD_DIM] + swapped * angle[:, HEAD_DIM:]).astype(jnp.bfloat16)

    kv_copy = pltpu.make_async_remote_copy(
        src_ref=kv_out.at[pl.ds(CORES, CORES)], dst_ref=kv_before, send_sem=kv_send,
        recv_sem=kv_recv, device_id=follower, device_id_type=MESH)

    def share_kv():
        for index in range(CORES):
            at = pl.ds(index * rows, rows)
            for begin in range(0, kv_per, HEAD_DIM):
                kv_out[CORES + index, :, pl.ds(begin, HEAD_DIM)] = turned(at, begin)
            kv_out[CORES + index, :, pl.ds(kv_per, kv_per)] = total[
                at, pl.ds(kv_per, kv_per)].astype(jnp.bfloat16)
        pl.when(plane < planes - 1)(lambda: kv_copy.start())

    def use(item):
        consume_guarded(*item)
        left[item[0]] -= 1
        if item[0] == 0 and left[0] == 0:
            share_kv()

    left = [sum(1 for event in events if event[0] == part) for part in range(3)]
    for part, offset in events:
        dz = offset[2]

        def arrive(part=part, offset=offset):
            own = block(part, offset)
            pltpu.make_async_remote_copy(
                src_ref=own, dst_ref=own, send_sem=block_send.at[0],
                recv_sem=block_recv.at[recv_index(part, offset)],
                device_id=partner, device_id_type=MESH).wait_recv()
        if dz:
            pl.when(inside(dz))(arrive)
        else:
            arrive()
        for hop in forwards(ORDERS[part], offset, depth):
            start(part, offset, hop)
        waiting.append((part, offset))
        if len(waiting) > lag and not ready:
            begin_products()
            ready = True
        if ready:
            for item in waiting[:2]:
                use(item)
            del waiting[:2]
    if not ready:
        begin_products()
    for item in waiting:
        use(item)
    for index in range(CORES):
        at = pl.ds(index * rows, rows)
        for begin in range(0, heads_per, HEAD_DIM):
            query_out[index, :, pl.ds(begin, HEAD_DIM)] = turned(at, 2 * kv_per + begin)
    for copy in others:
        copy.wait()
    meta_all[seq] = meta_ref[...]
    meta_out[...] = meta_all[...]

    @pl.when(plane > 0)
    def _():
        kv_copy.wait_recv()
        kv_out[0:CORES] = kv_before[...]

    @pl.when(plane == 0)
    def _():
        kv_out[0:CORES] = jnp.zeros_like(kv_before)

    pl.when(plane < planes - 1)(lambda: kv_copy.wait_send())
    for part, offset, hop in pending:
        guarded(offset, hop, lambda: send(part, offset, hop).wait_send())


def count_sends(depth):
    total = 0
    for order in ORDERS:
        for dz in range(1 - depth, depth):
            for dy in range(2):
                for dx in range(2):
                    total += len(forwards(order, (dx, dy, dz), depth))
    return total


def project(token_rows, qkv_weight, meta, turn):
    depth, n_seq = lax.axis_size("dp"), lax.axis_size("seq")
    rows, model = token_rows.shape
    columns = qkv_weight.shape[1]
    half = columns // CORES
    queries = HEADS // CORES * HEAD_DIM
    kv_width = half - queries
    chips = depth * n_seq // CORES
    block_rows = model // chips
    sends = count_sends(depth)
    recvs = len(ORDERS) * (2 * depth - 1) * 4
    vmem = pl.BlockSpec(memory_space=pltpu.VMEM)
    return pl.pallas_call(
        functools.partial(project_kernel, depth, n_seq),
        out_shape=(jax.ShapeDtypeStruct((CORES, rows, queries), jnp.bfloat16),
                   jax.ShapeDtypeStruct((2 * CORES, rows, kv_width), jnp.bfloat16),
                   jax.ShapeDtypeStruct((n_seq,) + meta.shape, jnp.int32)),
        in_specs=[pl.BlockSpec(memory_space=pl.ANY), pl.BlockSpec(memory_space=pl.ANY),
                  vmem, vmem],
        out_specs=(vmem, vmem, vmem),
        scratch_shapes=[
            pltpu.VMEM((CORES * rows, model), jnp.bfloat16),
            pltpu.VMEM((chips, block_rows, half), jnp.bfloat16),
            pltpu.VMEM((n_seq,) + meta.shape, jnp.int32),
            pltpu.VMEM((CORES * rows, 2 * HEAD_DIM), jnp.float32),
            pltpu.VMEM((CORES * rows, half), jnp.float32),
            pltpu.VMEM((CORES, rows, kv_width), jnp.bfloat16),
            pltpu.SemaphoreType.DMA((5,)),
            pltpu.SemaphoreType.DMA((5,)),
            pltpu.SemaphoreType.DMA((5,)),
            pltpu.SemaphoreType.DMA((n_seq,)),
            pltpu.SemaphoreType.DMA((n_seq,)),
            pltpu.SemaphoreType.DMA((sends,)),
            pltpu.SemaphoreType.DMA((recvs,)),
            pltpu.SemaphoreType.DMA,
            pltpu.SemaphoreType.DMA,
        ],
        compiler_params=pltpu.CompilerParams(
            collective_id=0, has_side_effects=True, vmem_limit_bytes=60 * 2**20),
        cost_estimate=pl.CostEstimate(flops=2 * rows * model * columns,
                                      bytes_accessed=2 * model * columns, transcendentals=0),
    )(token_rows, qkv_weight, meta, turn)


def project_plain(token_rows, qkv_weight, meta, turn):
    n_seq = lax.axis_size("seq")
    rows = token_rows.shape[0]
    core = lax.axis_index("seq") % CORES

    def paired(block):
        other = lax.ppermute(block, "seq", [(i, i ^ 1) for i in range(n_seq)])
        return jnp.where(core == 0, jnp.concatenate([block, other]),
                         jnp.concatenate([other, block]))

    weight = lax.all_gather(qkv_weight, ("dp", "seq"), axis=0, tiled=True)
    heads_per = HEADS // CORES * HEAD_DIM
    kv_per = KV_HEADS // CORES * HEAD_DIM
    pieces = [
        lax.dynamic_slice_in_dim(weight, base + core * width, width, 1)
        for base, width in ((0, heads_per), (HEADS * HEAD_DIM, kv_per),
                            ((HEADS + KV_HEADS) * HEAD_DIM, kv_per))
    ]
    projected = jnp.dot(paired(token_rows), jnp.concatenate(pieces, axis=1),
                        preferred_element_type=jnp.float32)
    angle = paired(turn)

    def turned(flat):
        heads = flat.reshape(flat.shape[0], -1, HEAD_DIM)
        swapped = jnp.roll(heads, HEAD_DIM // 2, axis=2)
        both = heads * angle[:, None, :HEAD_DIM] + swapped * angle[:, None, HEAD_DIM:]
        return both.reshape(flat.shape).astype(jnp.bfloat16)

    queries = turned(projected[:, :heads_per]).reshape(CORES, rows, heads_per)
    keys = turned(projected[:, heads_per : heads_per + kv_per])
    values = projected[:, heads_per + kv_per :].astype(jnp.bfloat16)
    own = jnp.concatenate([keys, values], axis=1)
    before = lax.ppermute(own, "seq", [(i, i + CORES) for i in range(n_seq - CORES)])
    span = jnp.concatenate([before, own]).reshape(2 * CORES, rows, 2 * kv_per)
    return queries, span, lax.all_gather(meta, "seq")


def turns(segment_ids, prefix_len):
    first_row = jnp.sum(
        (segment_ids[None, :] < segment_ids[:, None]).astype(jnp.int32), axis=1)
    index_list = jnp.arange(segment_ids.shape[0], dtype=jnp.int32)
    leading = first_row == 0
    position = index_list - first_row + jnp.where(leading, prefix_len, 0)
    half_dim = HEAD_DIM // 2
    frequency = ROPE_BASE ** (-2.0 * jnp.arange(half_dim, dtype=jnp.float32) / HEAD_DIM)
    angles = position.astype(jnp.float32)[:, None] * frequency[None, :]
    cosine, sine = jnp.cos(angles), jnp.sin(angles)
    return jnp.concatenate([cosine, cosine, -sine, sine], axis=1)


def attend_kernel(tile, metas_ref, pair_ref, q_ref, k_ref, v_ref, out_ref, rows_ref):
    block = pl.program_id(0)
    owner = lax.axis_index("seq") // CORES * CORES + block
    count = q_ref.shape[1]
    group = q_ref.shape[2] // HEAD_DIM
    prefix = metas_ref[owner, 2, 0]
    factor = HEAD_DIM ** -0.5 * 1.4426950408889634

    def run(index, remote):
        at = pl.ds(pl.multiple_of(index * tile, tile), tile)
        blocks = remote + 1
        window = pl.ds(block + REACH - remote, blocks)
        keys = k_ref[window].reshape(blocks * count, HEAD_DIM)
        values = v_ref[window].reshape(blocks * count, HEAD_DIM)
        row = pair_ref[owner, pl.ds(0, 1), :]
        columns = lax.broadcasted_iota(jnp.int32, (tile, count), 1)
        lines = lax.broadcasted_iota(jnp.int32, (tile, count), 0) + index * tile
        ids = jnp.sum(jnp.where(columns == lines, row, 0), axis=1, keepdims=True)
        seen = (columns <= lines) & (row == ids)
        if remote:
            back = lax.broadcasted_iota(jnp.int32, (tile, remote * count), 1) - remote * count
            lead = ids == row[:, :1]
            seen = jnp.concatenate([(back >= -prefix) & lead, seen], axis=1)
        parts = [pl.ds(head * HEAD_DIM, HEAD_DIM) for head in range(group)]
        queries = jnp.concatenate([q_ref[0, at, cols] for cols in parts], axis=0)
        scores = lax.dot_general(queries, keys, (((1,), (1,)), ((), ())),
                                 preferred_element_type=jnp.float32)
        scores = scores.reshape(group, tile, blocks * count)
        scores = jnp.where(seen[None], scores, MASKED)
        top = jnp.max(scores, axis=-1, keepdims=True)
        expo = jnp.exp2((scores - top) * factor)
        total = jnp.sum(expo, axis=-1, keepdims=True)
        out = jnp.dot(expo.astype(jnp.bfloat16).reshape(group * tile, blocks * count), values,
                      preferred_element_type=jnp.float32)
        out = (out.reshape(group, tile, HEAD_DIM) * (1.0 / total)).astype(jnp.bfloat16)
        for head, cols in enumerate(parts):
            rows_ref[at, cols] = out[head]

    @pl.loop(0, count // tile)
    def _(index):
        lead = metas_ref[owner, 0, index * tile] == metas_ref[owner, 0, 0]
        remote = jnp.where(lead, prefix, 0)
        for blocks in range(REACH + 1):
            low = remote > (blocks - 1) * count
            high = remote <= blocks * count
            cond = low & high if 0 < blocks < REACH else (high if blocks == 0 else low)
            pl.when(cond)(functools.partial(run, index, blocks))


    devices, _, capacity, width = out_ref.shape
    key = lax.broadcasted_iota(jnp.int32, (devices * capacity, count), 0)
    key = key // capacity * (CORES * capacity) + block * capacity + key % capacity
    chosen = jnp.where(key == pair_ref[owner, pl.ds(3, 1), :], 1.0, 0.0).astype(jnp.bfloat16)
    sent = jnp.dot(chosen, rows_ref[...], preferred_element_type=jnp.float32)
    out_ref[...] = sent.reshape(devices, 1, capacity, width).astype(jnp.bfloat16)


def attend(head, capacity, queries, span, metas):
    blocks, count, width = queries.shape
    n_seq = metas.shape[0]
    kv_heads = span.shape[2] // HEAD_DIM // 2
    group = width // kv_heads
    return pl.pallas_call(
        functools.partial(attend_kernel, count // 2),
        grid=(blocks,),
        out_shape=jax.ShapeDtypeStruct((n_seq, blocks, capacity, group), jnp.bfloat16),
        in_specs=[
            pl.BlockSpec(memory_space=pltpu.SMEM), pl.BlockSpec(memory_space=pltpu.VMEM),
            pl.BlockSpec((1, count, group), lambda b: (b, 0, head)),
            pl.BlockSpec((span.shape[0], count, HEAD_DIM), lambda b: (0, 0, head)),
            pl.BlockSpec((span.shape[0], count, HEAD_DIM), lambda b: (0, 0, kv_heads + head)),
        ],
        out_specs=pl.BlockSpec((n_seq, 1, capacity, group), lambda b: (0, b, 0, 0)),
        scratch_shapes=[pltpu.VMEM((count, group), jnp.bfloat16)],
        compiler_params=pltpu.CompilerParams(vmem_limit_bytes=60 * 2**20),
        cost_estimate=pl.CostEstimate(
            flops=4 * blocks * count * group * count * (REACH + 1),
            bytes_accessed=8 * blocks * count * group, transcendentals=0),
    )(metas, metas, queries, span, span)


def on_device(tokens, qkv_weight, segments, destination, doc_prefix):
    n_seq = lax.axis_size("seq")
    me = lax.axis_index("seq")
    count = tokens.shape[1]
    capacity = count // min(n_seq, 16)
    target = destination[0]
    owner = lax.div(target, count)
    index_list = jnp.arange(count, dtype=jnp.int32)
    earlier = (owner[None, :] == owner[:, None]) & (index_list[None, :] < index_list[:, None])
    core = lax.rem(me, CORES)
    slot = (owner * CORES + core) * capacity + jnp.sum(earlier.astype(jnp.int32), axis=1)
    prefix_row = jnp.broadcast_to(doc_prefix[0], (count,))
    meta = jnp.stack([segments[0], target, prefix_row, slot] + [slot] * (META_ROWS - 4))
    turn = turns(segments[0], doc_prefix[0, 0])
    planar = n_seq == 4 * CORES
    queries, span, metas = (project if planar else project_plain)(
        tokens[0], qkv_weight, meta, turn)
    kv_heads = KV_HEADS // CORES
    group = queries.shape[2] // kv_heads
    got = []
    for head in range(kv_heads):
        sent = attend(head, capacity, queries, span, metas)
        here = lax.all_to_all(sent.reshape(n_seq, CORES * capacity, group), "seq",
                              split_axis=0, concat_axis=0, tiled=True)
        got.append(here.reshape(n_seq // CORES, CORES, CORES, capacity, group))

    wanted = jnp.arange(CORES * capacity, dtype=jnp.int32).reshape(CORES, capacity)
    wanted = wanted + me * CORES * capacity
    wanted = jnp.tile(wanted, (n_seq // CORES, 1))
    match = metas[:, 3][:, None, :] == wanted[:, :, None]
    places = jnp.sum(
        jnp.where(match, lax.rem(metas[:, 1], count)[:, None, :] + 1, 0), axis=2) - 1
    places = places.reshape(-1)
    put = (index_list[:, None] == places[None, :]).astype(jnp.bfloat16)
    halves = [
        jnp.dot(put, got[head][:, c].reshape(n_seq * capacity, group),
                preferred_element_type=jnp.float32).astype(jnp.bfloat16)
        for c in range(CORES)
        for head in range(kv_heads)
    ]
    return jnp.concatenate(halves, axis=1)[None]


def solution(mesh):
    placed = (
        P("dp", "seq", None),
        P(("dp", "seq"), None),
        P("dp", "seq"),
        P("dp", "seq"),
        P("dp", "seq"),
    )
    return jax.shard_map(
        on_device, mesh=mesh, in_specs=placed, out_specs=P("dp", "seq", None), check_vma=False
    )
```
